128 devices in a mesh: ctx: 32 (over y, z, core), wt: 4 (over x).
Axes of the slice: x: 4, y: 4, z: 4, core: 2. Of those that a mesh axis runs over, the one named last changes fastest.
Arguments:
- layer_input: bfloat16 [4, 8192, 960], P('wt', 'ctx'), may hold values from -6 to 6
- doc_bounds: int32 [4, 2], P('wt'), may hold values from 1 to 8191, as said below
- attn_gain: bfloat16 [960], P('wt'), may hold values from 0.099609375 to 1.8984375
- w_query: bfloat16 [960, 960], P('wt'), may hold values from -0.1875 to 0.1875
- key_weight: bfloat16 [960, 320], P('wt'), may hold values from -0.1875 to 0.1875
- value_weight: bfloat16 [960, 320], P('wt'), may hold values from -0.1875 to 0.1875
- w_out: bfloat16 [960, 960], P('wt'), may hold values from -3.5 to 3.5
- mlp_gain: bfloat16 [960], P('wt'), may hold values from 0.099609375 to 1.8984375
- w_gate: bfloat16 [960, 2560], P('wt'), may hold values from -0.1875 to 0.1875
- w_up: bfloat16 [960, 2560], P('wt'), may hold values from -0.1875 to 0.1875
- w_down: bfloat16 [2560, 960], P('wt'), may hold values from -0.125 to 0.125
- cotangent: bfloat16 [4, 8192, 960], P('wt', 'ctx'), may hold values from -6 to 6
Outputs:
- layer_output: bfloat16 [4, 8192, 960], P('wt', 'ctx')
- input_grad: float32 [4, 8192, 960], P('wt', 'ctx')
- grad_attn_gain: float32 [960], P('wt')
- grad_w_query: float32 [960, 960], P('wt')
- grad_w_key: float32 [960, 320], P('wt')
- grad_w_value: float32 [960, 320], P('wt')
- grad_w_out: float32 [960, 960], P('wt')
- grad_mlp_gain: float32 [960], P('wt')
- grad_w_gate: float32 [960, 2560], P('wt')
- grad_w_up: float32 [960, 2560], P('wt')
- grad_w_down: float32 [2560, 960], P('wt')
The draws below stay inside these ranges and needn't reach their ends.
Inputs may be any that keep to these rules, and one draw needn't show every extreme that they name: `doc_bounds`: in every stream the first boundary lies among the first 128 tokens after token 0 and the second among the last 128 tokens, so the middle document spans the stream from its first device to its last.
All inputs are finite; a program needn't handle non-finite values.
Results may differ from the reference program's by a relative error of at most 0.03.
Values may be sent and summed in bfloat16 or wider, within the bound.
A program may use at most 128 MiB of HBM per device.

```python
import math
import jax
import jax.numpy as jnp
from jax import lax

MODEL_WIDTH = 960
QUERY_HEADS = 15
KEY_VALUE_HEADS = 5
HEAD_SIZE = 64
FF = 2560
BLK = 256
STREAMS = 4
STREAM_TOKENS = 8192


def draw_doc_bounds(key, part):
    key = jax.random.fold_in(key, 11)
    first_key, second_key = jax.random.split(key)
    first = jax.random.randint(first_key, (STREAMS, 1), 1, BLK // 2 + 1)
    second = STREAM_TOKENS - jax.random.randint(second_key, (STREAMS, 1), 1, BLK // 2 + 1)
    return jnp.concatenate([first, second], axis=1).astype(jnp.int32)


def block_levels(own_key, shape, pieces, low, largest):
    loudness, own = 1.0, jax.random.fold_in(own_key, 6)
    for position, shards_of in pieces:
        heights = jnp.exp(jax.random.uniform(jax.random.fold_in(own, position), (shards_of,), jnp.float32, low / len(pieces), largest / len(pieces)))
        loudness = loudness * jnp.repeat(heights, shape[position] // shards_of).reshape([-1 if axis == position else 1 for axis in range(len(shape))])
    return loudness


def centred(own_key, extent, width, reach, cuts=(), kind=jnp.bfloat16):
    entries = width * jax.random.normal(own_key, extent, jnp.float32)
    if cuts:
        entries = entries * block_levels(own_key, extent, cuts, -0.22, 0.18)
    return jnp.clip(entries, -reach, reach).astype(kind)


def setup_inputs(seed: int = 0) -> dict:
    streams_of = jax.random.split(jax.random.key(seed), 13)
    return {
        "layer_input": centred(streams_of[0], (STREAMS, STREAM_TOKENS, MODEL_WIDTH), 1.0, 6.0, ((0, 4), (1, 32))),
        "doc_bounds": draw_doc_bounds(jax.random.fold_in(streams_of[12], 71), 0),
        "attn_gain": jnp.clip(1.0 + 0.18 * jax.random.normal(streams_of[2], (MODEL_WIDTH,), jnp.float32), 0.099609375, 1.8984375).astype(jnp.bfloat16),
        "w_query": centred(streams_of[3], (MODEL_WIDTH, QUERY_HEADS * HEAD_SIZE), MODEL_WIDTH ** -0.5, 0.1875, ((0, 4),)),
        "key_weight": centred(streams_of[4], (MODEL_WIDTH, KEY_VALUE_HEADS * HEAD_SIZE), MODEL_WIDTH ** -0.5, 0.1875, ((0, 4),)),
        "value_weight": centred(streams_of[5], (MODEL_WIDTH, KEY_VALUE_HEADS * HEAD_SIZE), MODEL_WIDTH ** -0.5, 0.1875, ((0, 4),)),
        "w_out": centred(streams_of[6], (QUERY_HEADS * HEAD_SIZE, MODEL_WIDTH), (max(1, QUERY_HEADS * HEAD_SIZE // 256)) ** -0.5, 3.5, ((0, 4),)),
        "mlp_gain": jnp.clip(1.0 + 0.18 * jax.random.normal(streams_of[7], (MODEL_WIDTH,), jnp.float32), 0.099609375, 1.8984375).astype(jnp.bfloat16),
        "w_gate": centred(streams_of[8], (MODEL_WIDTH, FF), MODEL_WIDTH ** -0.5, 0.1875, ((0, 4),)),
        "w_up": centred(streams_of[9], (MODEL_WIDTH, FF), MODEL_WIDTH ** -0.5, 0.1875, ((0, 4),)),
        "w_down": centred(streams_of[10], (FF, MODEL_WIDTH), FF ** -0.5, 0.125, ((0, 4),)),
        "cotangent": centred(streams_of[11], (STREAMS, STREAM_TOKENS, MODEL_WIDTH), 1.0, 6.0, ((0, 4), (1, 32))),
    }


@jax.custom_vjp
def reduced_precision(v):
    return lax.optimization_barrier(v.astype(jnp.bfloat16)).astype(jnp.float32)

@jax.custom_vjp
def reduced_backward(v):
    return v

def low_keep(v):
    return (reduced_precision(v), None)

def low_pass(kept, grad):
    return (grad,)

def back_keep(v):
    return (v, None)

def back_low(kept, grad):
    return (reduced_precision(grad),)
reduced_precision.defvjp(low_keep, low_pass)
reduced_backward.defvjp(back_keep, back_low)
EPSILON = 1e-05
HIGHEST = lax.Precision.HIGHEST

def matrix_product(left, right):
    return jnp.dot(left, right, precision=HIGHEST, preferred_element_type=jnp.float32)

def rms_scale(values, gain):
    inverse = lax.rsqrt(lax.optimization_barrier(jnp.mean(values * values, axis=-1, keepdims=True)) + EPSILON)
    return values * inverse * gain

def tables(positions):
    half = HEAD_SIZE // 2
    freqs = 10000.0 ** (-jnp.arange(half, dtype=jnp.float32) * 2.0 / HEAD_SIZE)
    angles = positions.astype(jnp.float32)[:, None] * freqs[None, :]
    angles = jnp.concatenate([angles, angles], axis=-1)
    return (jnp.cos(angles)[:, None, :], jnp.sin(angles)[:, None, :])

def rotate(values, cosine_table, sine_table):
    half = values.shape[-1] // 2
    turned = jnp.concatenate([-values[..., half:], values[..., :half]], axis=-1)
    return values * cosine_table + turned * sine_table

def layout(doc_edges):
    token_index = jnp.arange(STREAM_TOKENS, dtype=jnp.int32)
    segment = (token_index >= doc_edges[0]).astype(jnp.int32) + (token_index >= doc_edges[1]).astype(jnp.int32)
    starts = jnp.where(segment == 0, 0, jnp.where(segment == 1, doc_edges[0], doc_edges[1]))
    return (token_index, segment, token_index - starts)

def attend(query_rows, key_row_set, value_row_set, token_index, segment):
    group_count = QUERY_HEADS // KEY_VALUE_HEADS
    block_length = math.gcd(STREAM_TOKENS, 512)
    count_of_blocks = STREAM_TOKENS // block_length
    query_block_set = query_rows.reshape(count_of_blocks, block_length, KEY_VALUE_HEADS, group_count, HEAD_SIZE)
    index_blocks = token_index.reshape(count_of_blocks, block_length)
    segment_blocks = segment.reshape(count_of_blocks, block_length)

    def one_block(items):
        query_part, index_part, segment_part = items
        scores = jnp.einsum('qjgd,kjd->jgqk', query_part, key_row_set, precision=HIGHEST) * HEAD_SIZE ** (-0.5)
        scores = reduced_backward(scores)
        visible = (token_index[None, :] <= index_part[:, None]) & (segment[None, :] == segment_part[:, None])
        scores = jnp.where(visible[None, None], scores, -1e+30)
        weights_soft = reduced_precision(jax.nn.softmax(scores, axis=-1))
        return jnp.einsum('jgqk,kjd->qjgd', weights_soft, value_row_set, precision=HIGHEST)
    result = lax.map(jax.checkpoint(one_block), (query_block_set, index_blocks, segment_blocks))
    return result.reshape(STREAM_TOKENS, QUERY_HEADS * HEAD_SIZE)

def forward(layer_in, doc_edges, attn_gain, w_query, key_weight, value_weight, w_out, mlp_gain, w_gate, w_up, w_down):
    token_index, segment, positions = layout(doc_edges)
    cosine_table, sine_table = tables(positions)
    normalized = reduced_precision(rms_scale(layer_in, attn_gain))
    query_rows = reduced_backward(matrix_product(normalized, w_query)).reshape(STREAM_TOKENS, QUERY_HEADS, HEAD_SIZE)
    key_row_set = reduced_backward(matrix_product(normalized, key_weight)).reshape(STREAM_TOKENS, KEY_VALUE_HEADS, HEAD_SIZE)
    value_row_set = reduced_precision(reduced_backward(matrix_product(normalized, value_weight))).reshape(STREAM_TOKENS, KEY_VALUE_HEADS, HEAD_SIZE)
    query_rows = reduced_precision(rotate(query_rows, cosine_table, sine_table))
    key_row_set = reduced_precision(rotate(key_row_set, cosine_table, sine_table))
    mixed = reduced_precision(reduced_backward(attend(query_rows, key_row_set, value_row_set, token_index, segment)))
    resid = layer_in + reduced_backward(matrix_product(mixed, w_out))
    normed_two = reduced_precision(rms_scale(resid, mlp_gain))
    gate_pre = reduced_backward(matrix_product(normed_two, w_gate))
    up_part = reduced_backward(matrix_product(normed_two, w_up))
    hidden = reduced_precision(jax.nn.silu(gate_pre) * up_part)
    return resid + reduced_backward(matrix_product(hidden, w_down))

def reference(layer_input, doc_bounds, attn_gain, w_query, key_weight, value_weight, w_out, mlp_gain, w_gate, w_up, w_down, cotangent):
    params = tuple((weight.astype(jnp.float32) for weight in (attn_gain, w_query, key_weight, value_weight, w_out, mlp_gain, w_gate, w_up, w_down)))

    def stream_step(totals, items):
        stream_in, stream_edges, stream_cot = items

        def local(layer_in, *weights):
            return forward(layer_in, stream_edges, *weights)
        output, pullback = jax.vjp(local, stream_in.astype(jnp.float32), *params)
        gradients = pullback(stream_cot.astype(jnp.float32))
        totals = tuple((first + second for first, second in zip(totals, gradients[1:])))
        return (totals, (output.astype(jnp.bfloat16), gradients[0]))
    zero_filled = tuple((jnp.zeros_like(weight) for weight in params))
    totals, (outputs, input_grads) = lax.scan(stream_step, zero_filled, (layer_input, doc_bounds, cotangent))
    return (outputs, input_grads, totals[0], totals[1], totals[2], totals[3], totals[4], totals[5], totals[6], totals[7], totals[8])
```

```python
import functools

import jax
import jax.numpy as jnp
from jax import lax
from jax.experimental import pallas as pl
from jax.experimental.pallas import tpu as pltpu
from jax.sharding import PartitionSpec as P

QUERY_HEADS = 15
KEY_VALUE_HEADS = 5
HEAD_SIZE = 64
GROUP = QUERY_HEADS // KEY_VALUE_HEADS
PAIR = 2 * HEAD_SIZE
EPSILON = 1e-05
NEG = -1e30
BIG = 1e30
LOG2E = 1.4426950408889634
F32 = jnp.float32
BF16 = jnp.bfloat16
HEAD_SETS = ((0, KEY_VALUE_HEADS),)


def dot_f32(left, right, dims=((1,), (0,))):
    return lax.dot_general(left, right, (dims, ((), ())), preferred_element_type=F32)


def ranges(me, half):
    light = me < half
    first = jnp.where(light, 0, me - half + 1)
    mirrored = jnp.where(light, half - me, 0)
    return first, mirrored


def visible_pairs(b0, b1, key_start, query_start, rows):
    key = key_start + lax.broadcasted_iota(jnp.int32, (rows, rows), 0)
    query = query_start + lax.broadcasted_iota(jnp.int32, (rows, rows), 1)
    return (key <= query) & ((key >= b0) | (query < b0)) & ((key >= b1) | (query < b1))


def sweep(me, n, step):
    first, mirrored = ranges(me, n // 2)
    step_own = lambda block, masked, diagonal: step(0, block, masked, diagonal)

    @pl.when((first == 0) & (me > 0))
    def _():
        step_own(0, True, False)

    def own(block, carry):
        step_own(block, False, False)
        return carry

    lax.fori_loop(jnp.maximum(first, 1), me, own, 0)
    step_own(me, True, True)

    @pl.when(mirrored > 0)
    def _():
        step(1, 0, True, False)

        def other(block, carry):
            step(1, block, False, False)
            return carry

        lax.fori_loop(1, mirrored, other, 0)


def forward_kernel(n, place, kv_ref, q_ref, o_ref, stat_ref, peak, mass, total):
    me, b0, b1 = place[0], place[1], place[2]
    rows = q_ref.shape[-1]
    peak[...] = jnp.full_like(peak, NEG)
    mass[...] = jnp.zeros_like(mass)
    total[...] = jnp.zeros_like(total)

    def step(which, block, masked, diagonal):
        kv = kv_ref[block]
        v_turned = kv.T[HEAD_SIZE:]
        if diagonal:
            query = me * rows + lax.broadcasted_iota(jnp.int32, (1, rows), 1)
            fresh = query >= b1
            for g in range(GROUP):
                peak[which, g] = jnp.where(fresh, NEG, peak[which, g])
                mass[which, g] = jnp.where(fresh, 0.0, mass[which, g])
                total[which, g] = jnp.where(fresh, 0.0, total[which, g])
        if masked:
            owner = me if which == 0 else n - 1 - me
            seen = visible_pairs(b0, b1, block * rows, owner * rows, rows)
        for g in range(GROUP):
            scores = dot_f32(kv, q_ref[which, g])
            if masked:
                scores = jnp.where(seen, scores, NEG)
            old = peak[which, g]
            new = jnp.maximum(old, jnp.max(scores, axis=0, keepdims=True))
            weights = jnp.exp2((scores - new) * LOG2E)
            factor = jnp.exp2((old - new) * LOG2E)
            peak[which, g] = new
            mass[which, g] = mass[which, g] * factor + jnp.sum(weights, axis=0, keepdims=True)
            total[which, g] = total[which, g] * factor + dot_f32(v_turned, weights.astype(BF16))

    sweep(me, n, step)
    for which in range(2):
        for g in range(GROUP):
            held = mass[which, g]
            live = held > 0.0
            safe = jnp.where(live, held, 1.0)
            o_ref[which, g] = total[which, g] / safe
            stat_ref[which, g] = jnp.where(live, peak[which, g] + jnp.log(safe), NEG)


def backward_kernel(n, place, kv_ref, q_ref, do_ref, q_flat, do_flat, stat_ref, dq_ref, dkv_ref, gathered):
    me, b0, b1 = place[0], place[1], place[2]
    rows = q_ref.shape[-1]
    half = n // 2
    first, _ = ranges(me, half)
    gathered[...] = jnp.zeros_like(gathered)
    dq_ref[...] = jnp.zeros_like(dq_ref)

    def step(which, block, masked, diagonal):
        kv = kv_ref[block]
        k_turned = kv.T[:HEAD_SIZE]
        stats = 2 if diagonal else which
        if masked:
            owner = me if which == 0 else n - 1 - me
            seen = visible_pairs(b0, b1, block * rows, owner * rows, rows)
        more = jnp.zeros((rows, PAIR), F32)
        for g in range(GROUP):
            scores = dot_f32(kv, q_ref[which, g])
            weights = jnp.exp2((scores - stat_ref[stats, g, 0:1]) * LOG2E)
            if masked:
                weights = jnp.where(seen, weights, 0.0)
            weight_grad = dot_f32(kv, do_ref[which, g])
            score_grad = (weights * (weight_grad - stat_ref[stats, g, 1:2])).astype(BF16)
            more += dot_f32(score_grad, q_flat[which, g])
            more += dot_f32(weights.astype(BF16), do_flat[which, g])
            dq_ref[which, g] += dot_f32(k_turned, score_grad)
        gathered[block - first] += more

    sweep(me, n, step)
    for block in range(n):
        slot = block - first
        inside = (slot >= 0) & (slot < half)

        @pl.when(inside)
        def _():
            dkv_ref[block] = gathered[slot].astype(BF16)

        @pl.when(jnp.logical_not(inside))
        def _():
            dkv_ref[block] = jnp.zeros(dkv_ref.shape[1:], BF16)


def whole_set(per_head):
    return pl.BlockSpec(per_head, lambda j: (0, j) + (0,) * (len(per_head) - 2))


def attention_forward(n, place, kv, q_turned):
    heads, rows = kv.shape[0], kv.shape[2]
    units = (n + 1) * heads
    return pl.pallas_call(
        functools.partial(forward_kernel, n),
        grid=(heads,),
        out_shape=(
            jax.ShapeDtypeStruct((2, heads * GROUP, HEAD_SIZE, rows), F32),
            jax.ShapeDtypeStruct((2, heads * GROUP, 1, rows), F32),
        ),
        in_specs=[
            pl.BlockSpec(memory_space=pltpu.SMEM),
            pl.BlockSpec((None, n, rows, PAIR), lambda j: (j, 0, 0, 0)),
            whole_set((2, GROUP, PAIR, rows)),
        ],
        out_specs=(whole_set((2, GROUP, HEAD_SIZE, rows)), whole_set((2, GROUP, 1, rows))),
        scratch_shapes=[
            pltpu.VMEM((2, GROUP, 1, rows), F32),
            pltpu.VMEM((2, GROUP, 1, rows), F32),
            pltpu.VMEM((2, GROUP, HEAD_SIZE, rows), F32),
        ],
        compiler_params=pltpu.CompilerParams(vmem_limit_bytes=40 * 2**20),
        cost_estimate=pl.CostEstimate(
            flops=units * GROUP * rows * rows * 4 * PAIR,
            bytes_accessed=2 * n * rows * PAIR * heads,
            transcendentals=units * GROUP * rows * rows,
        ),
        name="attend_forward",
    )(place, kv, q_turned)


def attention_backward(n, place, kv, q_turned, do_turned, q_flat, do_flat, stats):
    heads, rows = kv.shape[0], kv.shape[2]
    units = (n + 1) * heads
    return pl.pallas_call(
        functools.partial(backward_kernel, n),
        grid=(heads,),
        out_shape=(
            jax.ShapeDtypeStruct((2, heads * GROUP, HEAD_SIZE, rows), F32),
            jax.ShapeDtypeStruct((heads, n, rows, PAIR), BF16),
        ),
        in_specs=[
            pl.BlockSpec(memory_space=pltpu.SMEM),
            pl.BlockSpec((None, n, rows, PAIR), lambda j: (j, 0, 0, 0)),
            whole_set((2, GROUP, PAIR, rows)),
            whole_set((2, GROUP, PAIR, rows)),
            whole_set((2, GROUP, rows, PAIR)),
            whole_set((2, GROUP, rows, PAIR)),
            whole_set((3, GROUP, 2, rows)),
        ],
        out_specs=(
            whole_set((2, GROUP, HEAD_SIZE, rows)),
            pl.BlockSpec((None, n, rows, PAIR), lambda j: (j, 0, 0, 0)),
        ),
        scratch_shapes=[pltpu.VMEM((n // 2, rows, PAIR), F32)],
        compiler_params=pltpu.CompilerParams(vmem_limit_bytes=40 * 2**20),
        cost_estimate=pl.CostEstimate(
            flops=units * GROUP * rows * rows * 10 * PAIR,
            bytes_accessed=4 * n * rows * PAIR * heads,
            transcendentals=units * GROUP * rows * rows,
        ),
        name="attend_backward",
    )(place, kv, q_turned, do_turned, q_flat, do_flat, stats)


def rms_forward(values, gain):
    inverse = lax.rsqrt(jnp.mean(values * values, axis=-1, keepdims=True) + EPSILON)
    normal = values * inverse
    return (normal * gain, normal, inverse)


def rms_backward(upstream, gain, normal, inverse):
    scaled = upstream * gain
    inner = jnp.mean(scaled * normal, axis=-1, keepdims=True)
    return (inverse * (scaled - normal * inner), jnp.sum(upstream * normal, axis=0))


def positions_of(edges, me, rows):
    token = me * rows + jnp.arange(rows, dtype=jnp.int32)
    start = jnp.where(token >= edges[1], edges[1], jnp.where(token >= edges[0], edges[0], 0))
    return token, token - start


def turn(heads, cosine, sine):
    half = HEAD_SIZE // 2
    low, high = heads[:, :half], heads[:, half:]
    return jnp.concatenate([low * cosine - high * sine, high * cosine + low * sine], axis=1)


def turn_back(heads, cosine, sine):
    half = HEAD_SIZE // 2
    low, high = heads[:, :half], heads[:, half:]
    return jnp.concatenate([low * cosine + high * sine, high * cosine - low * sine], axis=1)


def three_parts(values):
    first = lax.reduce_precision(values, 8, 7)
    rest = values - first
    second = lax.reduce_precision(rest, 8, 7)
    third = rest - second
    return [part.astype(BF16) for part in (first, second, third)]


def joined(parts):
    return parts[0].astype(F32) + parts[1].astype(F32) + parts[2].astype(F32)


def gather_weight(shard):
    return lax.all_gather(shard, "wt", axis=0, tiled=True)


def reduce_gradient(gradient):
    part = lax.psum_scatter(gradient.astype(BF16), "wt", scatter_dimension=0, tiled=True)
    return lax.psum(part, "ctx").astype(F32)


def per_device(
    layer_input,
    doc_bounds,
    attn_gain,
    w_query,
    key_weight,
    value_weight,
    w_out,
    mlp_gain,
    w_gate,
    w_up,
    w_down,
    cotangent,
):
    n = lax.axis_size("ctx")
    me = lax.axis_index("ctx")
    rows, width = layer_input.shape[1:]
    queries = QUERY_HEADS * HEAD_SIZE
    keys = KEY_VALUE_HEADS * HEAD_SIZE
    edges = doc_bounds[0]
    place = jnp.concatenate([jnp.full((1,), me, jnp.int32), edges])
    across = [(i, n - 1 - i) for i in range(n)]

    gains = jnp.pad(jnp.stack([attn_gain, mlp_gain], axis=1), ((0, 0), (0, 62)))
    shard_qkv = jnp.concatenate([w_query, key_weight, value_weight, gains], axis=1)
    full_qkv = gather_weight(shard_qkv)
    gain_rows = full_qkv[:, queries + 2 * keys : queries + 2 * keys + 2].T.astype(F32)
    attn_scale, mlp_scale = gain_rows[0], gain_rows[1]
    full_qkv = full_qkv[:, : queries + 2 * keys]

    x = layer_input[0].astype(F32)
    normed, normal_in, inverse_in = rms_forward(x, attn_scale)
    normed = normed.astype(BF16)
    turned = dot_f32(full_qkv, normed, ((0,), (1,)))
    token, position = positions_of(edges, me, rows)
    freqs = 10000.0 ** (-jnp.arange(HEAD_SIZE // 2, dtype=F32) * 2.0 / HEAD_SIZE)
    angles = freqs[:, None] * position.astype(F32)[None, :]
    cosine, sine = jnp.cos(angles), jnp.sin(angles)

    q = turn(turned[:queries].reshape(QUERY_HEADS, HEAD_SIZE, rows), cosine, sine).astype(BF16)
    k = turn(turned[queries : queries + keys].reshape(KEY_VALUE_HEADS, HEAD_SIZE, rows), cosine, sine).astype(BF16)
    v = turned[queries + keys :].reshape(KEY_VALUE_HEADS, HEAD_SIZE, rows).astype(BF16)
    q = q * BF16(HEAD_SIZE**-0.5)
    own_kv = jnp.concatenate([k, v], axis=1).transpose(0, 2, 1)

    kv_sets = [lax.all_gather(own_kv[j : j + c], "ctx", axis=1) for j, c in HEAD_SETS]
    q_both = jnp.stack([q, lax.ppermute(q, "ctx", across)])
    blank = jnp.zeros_like(q_both)
    q_turned = jnp.concatenate([q_both, blank], axis=2)
    q_flat = q_turned.transpose(0, 1, 3, 2)

    later = token >= edges[1]
    own_o, own_stat = [], []
    for (j, c), kv in zip(HEAD_SETS, kv_sets):
        some = slice(j * GROUP, (j + c) * GROUP)
        o_part, stat_part = attention_forward(n, place, kv, q_turned[:, some])
        sent = jnp.concatenate([o_part[1].astype(BF16)] + three_parts(stat_part[1]) , axis=1)
        got = lax.ppermute(sent, "ctx", across)
        other_stat = joined([got[:, HEAD_SIZE + i : HEAD_SIZE + i + 1] for i in range(3)])
        other_stat = jnp.where(later, NEG, other_stat)
        stat = jnp.logaddexp(stat_part[0], other_stat)
        own_o.append(
            o_part[0] * jnp.exp(stat_part[0] - stat)
            + got[:, :HEAD_SIZE].astype(F32) * jnp.exp(other_stat - stat)
        )
        own_stat.append(stat)
    attended = jnp.concatenate(own_o)
    log_total = jnp.concatenate(own_stat)
    mixed = attended.reshape(queries, rows).astype(BF16)

    full_out = gather_weight(w_out)
    full_gate = gather_weight(w_gate)
    full_up = gather_weight(w_up)
    full_down = gather_weight(w_down)
    resid = x + dot_f32(mixed, full_out, ((0,), (0,)))
    normed_two, normal_mlp, inverse_mlp = rms_forward(resid, mlp_scale)
    normed_two = normed_two.astype(BF16)
    gate = dot_f32(normed_two, full_gate)
    up = dot_f32(normed_two, full_up)
    sig = jax.nn.sigmoid(gate)
    activated = gate * sig
    hidden = (activated * up).astype(BF16)
    layer_output = (resid + dot_f32(hidden, full_down)).astype(BF16)[None]
    upstream = cotangent[0]
    grad_w_down = dot_f32(hidden, upstream, ((0,), (0,)))
    grad_hidden = dot_f32(upstream, full_down, ((1,), (1,)))
    grad_up_in = (grad_hidden * activated).astype(BF16)
    grad_gate_in = (grad_hidden * up * sig * (1.0 + gate * (1.0 - sig))).astype(BF16)
    grad_w_gate = dot_f32(normed_two, grad_gate_in, ((0,), (0,)))
    grad_w_up = dot_f32(normed_two, grad_up_in, ((0,), (0,)))
    grad_normed_two = dot_f32(grad_gate_in, full_gate, ((1,), (1,))) + dot_f32(
        grad_up_in, full_up, ((1,), (1,))
    )
    grad_resid_mlp, grad_mlp_gain = rms_backward(grad_normed_two, mlp_scale, normal_mlp, inverse_mlp)
    grad_resid = upstream.astype(F32) + grad_resid_mlp
    grad_mixed = grad_resid.astype(BF16)
    grad_w_out = dot_f32(mixed, grad_mixed)
    grad_attended = dot_f32(full_out, grad_mixed, ((1,), (1,))).astype(BF16)
    grad_attended = grad_attended.reshape(QUERY_HEADS, HEAD_SIZE, rows)
    grad_dot = jnp.sum(grad_attended.astype(F32) * attended, axis=1, keepdims=True)

    before = jnp.where(later, BIG, log_total)
    sent = jnp.concatenate([grad_attended] + three_parts(before) + three_parts(grad_dot), axis=1)
    got = lax.ppermute(sent, "ctx", across)
    piece = lambda i: got[:, HEAD_SIZE + i : HEAD_SIZE + i + 1]
    stats = jnp.stack(
        [
            jnp.concatenate([before, grad_dot], axis=1),
            jnp.concatenate([joined([piece(0), piece(1), piece(2)]), joined([piece(3), piece(4), piece(5)])], axis=1),
            jnp.concatenate([log_total, grad_dot], axis=1),
        ]
    )
    do_both = jnp.stack([grad_attended, got[:, :HEAD_SIZE]])
    do_turned = jnp.concatenate([blank, do_both], axis=2)
    do_flat = do_turned.transpose(0, 1, 3, 2)
    dq_all, dkv_all = [], []
    for (j, c), kv in zip(HEAD_SETS, kv_sets):
        some = slice(j * GROUP, (j + c) * GROUP)
        dq, dkv = attention_backward(
            n, place, kv, q_turned[:, some], do_turned[:, some], q_flat[:, some], do_flat[:, some], stats[:, some]
        )
        other = lax.ppermute(dq[1].astype(BF16), "ctx", across)
        dq_all.append(dq[0] + other.astype(F32))
        dkv_all.append(lax.psum_scatter(dkv, "ctx", scatter_dimension=1, tiled=False))
    grad_q = turn_back(jnp.concatenate(dq_all) * HEAD_SIZE**-0.5, cosine, sine).astype(BF16)
    dkv = jnp.concatenate(dkv_all).astype(F32).transpose(0, 2, 1)
    grad_k = turn_back(dkv[:, :HEAD_SIZE], cosine, sine).astype(BF16)
    grad_v = dkv[:, HEAD_SIZE:].astype(BF16)
    grad_qkv = jnp.concatenate(
        [grad_q.reshape(queries, rows), grad_k.reshape(keys, rows), grad_v.reshape(keys, rows)]
    )
    grad_w_qkv = dot_f32(normed, grad_qkv, ((0,), (1,)))
    grad_normed = dot_f32(grad_qkv, full_qkv, ((0,), (1,)))
    grad_in, grad_attn_gain = rms_backward(grad_normed, attn_scale, normal_in, inverse_in)
    input_grad = (grad_resid + grad_in)[None]

    sum_qkv = reduce_gradient(grad_w_qkv)
    gain_sum = lax.psum(jnp.stack([grad_attn_gain, grad_mlp_gain]).astype(BF16), ("wt", "ctx"))
    mine = lax.dynamic_slice_in_dim(gain_sum, lax.axis_index("wt") * attn_gain.shape[0], attn_gain.shape[0], 1)
    mine = mine.astype(F32)
    return (
        layer_output,
        input_grad,
        mine[0],
        sum_qkv[:, :queries],
        sum_qkv[:, queries : queries + keys],
        sum_qkv[:, queries + keys :],
        reduce_gradient(grad_w_out),
        mine[1],
        reduce_gradient(grad_w_gate),
        reduce_gradient(grad_w_up),
        reduce_gradient(grad_w_down),
    )


def solution(mesh):
    tokens, weights, gains = P("wt", "ctx", None), P("wt", None), P("wt")
    return jax.shard_map(
        per_device,
        mesh=mesh,
        in_specs=(
            tokens, weights, gains, weights, weights, weights, weights, gains, weights, weights, weights, tokens,
        ),
        out_specs=(
            tokens, tokens, gains, weights, weights, weights, weights, gains, weights, weights, weights,
        ),
        check_vma=False,
    )
```

```python
import functools

import jax
import jax.numpy as jnp
from jax import lax
from jax.experimental import pallas as pl
from jax.experimental.pallas import tpu as pltpu
from jax.sharding import PartitionSpec as P

QUERY_HEADS = 15
KEY_VALUE_HEADS = 5
HEAD_SIZE = 64
GROUP = QUERY_HEADS // KEY_VALUE_HEADS
PAIR = 2 * HEAD_SIZE
EPSILON = 1e-05
NEG = -1e30
BIG = 1e30
LOG2E = 1.4426950408889634
F32 = jnp.float32
BF16 = jnp.bfloat16


def dot_f32(left, right, dims=((1,), (0,))):
    return lax.dot_general(left, right, (dims, ((), ())), preferred_element_type=F32)


def ranges(me, half):
    light = me < half
    first = jnp.where(light, 0, me - half + 1)
    mirrored = jnp.where(light, half - me, 0)
    return first, mirrored


def visible_pairs(b0, b1, key_start, query_start, rows):
    key = key_start + lax.broadcasted_iota(jnp.int32, (rows, rows), 0)
    query = query_start + lax.broadcasted_iota(jnp.int32, (rows, rows), 1)
    return (key <= query) & ((key >= b0) | (query < b0)) & ((key >= b1) | (query < b1))


def sweep(me, n, step):
    first, mirrored = ranges(me, n // 2)
    step_own = lambda block, masked, diagonal: step(0, block, masked, diagonal)

    @pl.when((first == 0) & (me > 0))
    def _():
        step_own(0, True, False)

    def own(block, carry):
        step_own(block, False, False)
        return carry

    lax.fori_loop(jnp.maximum(first, 1), me, own, 0)
    step_own(me, True, True)

    @pl.when(mirrored > 0)
    def _():
        step(1, 0, True, False)

        def other(block, carry):
            step(1, block, False, False)
            return carry

        lax.fori_loop(1, mirrored, other, 0)


def forward_kernel(n, place, kv_ref, q_ref, o_ref, stat_ref, peak, mass, total):
    me, b0, b1 = place[0], place[1], place[2]
    rows = q_ref.shape[-1]
    peak[...] = jnp.full_like(peak, NEG)
    mass[...] = jnp.zeros_like(mass)
    total[...] = jnp.zeros_like(total)

    def step(which, block, masked, diagonal):
        kv = kv_ref[block]
        v_turned = kv.T[HEAD_SIZE:]
        if diagonal:
            query = me * rows + lax.broadcasted_iota(jnp.int32, (1, rows), 1)
            fresh = query >= b1
            for g in range(GROUP):
                peak[which, g] = jnp.where(fresh, NEG, peak[which, g])
                mass[which, g] = jnp.where(fresh, 0.0, mass[which, g])
                total[which, g] = jnp.where(fresh, 0.0, total[which, g])
        if masked:
            owner = me if which == 0 else n - 1 - me
            seen = visible_pairs(b0, b1, block * rows, owner * rows, rows)
        for g in range(GROUP):
            scores = dot_f32(kv, q_ref[which, g])
            if masked:
                scores = jnp.where(seen, scores, NEG)
            old = peak[which, g]
            new = jnp.maximum(old, jnp.max(scores, axis=0, keepdims=True))
            weights = jnp.exp2((scores - new) * LOG2E)
            factor = jnp.exp2((old - new) * LOG2E)
            peak[which, g] = new
            mass[which, g] = mass[which, g] * factor + jnp.sum(weights, axis=0, keepdims=True)
            total[which, g] = total[which, g] * factor + dot_f32(v_turned, weights.astype(BF16))

    sweep(me, n, step)
    for which in range(2):
        for g in range(GROUP):
            held = mass[which, g]
            live = held > 0.0
            safe = jnp.where(live, held, 1.0)
            o_ref[which, g] = total[which, g] / safe
            stat_ref[which, g] = jnp.where(live, peak[which, g] + jnp.log(safe), NEG)


def backward_kernel(n, place, kv_ref, q_ref, do_ref, q_flat, do_flat, stat_ref, dq_ref, dkv_ref, gathered):
    me, b0, b1 = place[0], place[1], place[2]
    rows = q_ref.shape[-1]
    half = n // 2
    first, _ = ranges(me, half)
    gathered[...] = jnp.zeros_like(gathered)
    dq_ref[...] = jnp.zeros_like(dq_ref)

    def step(which, block, masked, diagonal):
        kv = kv_ref[block]
        k_turned = kv.T[:HEAD_SIZE]
        stats = 2 if diagonal else which
        if masked:
            owner = me if which == 0 else n - 1 - me
            seen = visible_pairs(b0, b1, block * rows, owner * rows, rows)
        more = jnp.zeros((rows, PAIR), F32)
        for g in range(GROUP):
            scores = dot_f32(kv, q_ref[which, g])
            weights = jnp.exp2((scores - stat_ref[stats, g, 0:1]) * LOG2E)
            if masked:
                weights = jnp.where(seen, weights, 0.0)
            weight_grad = dot_f32(kv, do_ref[which, g])
            score_grad = (weights * (weight_grad - stat_ref[stats, g, 1:2])).astype(BF16)
            more += dot_f32(score_grad, q_flat[which, g])
            more += dot_f32(weights.astype(BF16), do_flat[which, g])
            dq_ref[which, g] += dot_f32(k_turned, score_grad)
        gathered[block - first] += more

    sweep(me, n, step)
    for block in range(n):
        slot = block - first
        inside = (slot >= 0) & (slot < half)

        @pl.when(inside)
        def _():
            dkv_ref[block] = gathered[slot].astype(BF16)

        @pl.when(jnp.logical_not(inside))
        def _():
            dkv_ref[block] = jnp.zeros(dkv_ref.shape[1:], BF16)


def whole_set(per_head):
    return pl.BlockSpec(per_head, lambda j: (0, j) + (0,) * (len(per_head) - 2))


def attention_forward(n, place, kv, q_turned):
    heads, rows = kv.shape[0], kv.shape[2]
    units = (n + 1) * heads
    return pl.pallas_call(
        functools.partial(forward_kernel, n),
        grid=(heads,),
        out_shape=(
            jax.ShapeDtypeStruct((2, heads * GROUP, HEAD_SIZE, rows), F32),
            jax.ShapeDtypeStruct((2, heads * GROUP, 1, rows), F32),
        ),
        in_specs=[
            pl.BlockSpec(memory_space=pltpu.SMEM),
            pl.BlockSpec((None, n, rows, PAIR), lambda j: (j, 0, 0, 0)),
            whole_set((2, GROUP, PAIR, rows)),
        ],
        out_specs=(whole_set((2, GROUP, HEAD_SIZE, rows)), whole_set((2, GROUP, 1, rows))),
        scratch_shapes=[
            pltpu.VMEM((2, GROUP, 1, rows), F32),
            pltpu.VMEM((2, GROUP, 1, rows), F32),
            pltpu.VMEM((2, GROUP, HEAD_SIZE, rows), F32),
        ],
        compiler_params=pltpu.CompilerParams(vmem_limit_bytes=40 * 2**20),
        cost_estimate=pl.CostEstimate(
            flops=units * GROUP * rows * rows * 4 * PAIR,
            bytes_accessed=2 * n * rows * PAIR * heads,
            transcendentals=units * GROUP * rows * rows,
        ),
        name="attend_forward",
    )(place, kv, q_turned)


def attention_backward(n, place, kv, q_turned, do_turned, q_flat, do_flat, stats):
    heads, rows = kv.shape[0], kv.shape[2]
    units = (n + 1) * heads
    return pl.pallas_call(
        functools.partial(backward_kernel, n),
        grid=(heads,),
        out_shape=(
            jax.ShapeDtypeStruct((2, heads * GROUP, HEAD_SIZE, rows), F32),
            jax.ShapeDtypeStruct((heads, n, rows, PAIR), BF16),
        ),
        in_specs=[
            pl.BlockSpec(memory_space=pltpu.SMEM),
            pl.BlockSpec((None, n, rows, PAIR), lambda j: (j, 0, 0, 0)),
            whole_set((2, GROUP, PAIR, rows)),
            whole_set((2, GROUP, PAIR, rows)),
            whole_set((2, GROUP, rows, PAIR)),
            whole_set((2, GROUP, rows, PAIR)),
            whole_set((3, GROUP, 2, rows)),
        ],
        out_specs=(
            whole_set((2, GROUP, HEAD_SIZE, rows)),
            pl.BlockSpec((None, n, rows, PAIR), lambda j: (j, 0, 0, 0)),
        ),
        scratch_shapes=[pltpu.VMEM((n // 2, rows, PAIR), F32)],
        compiler_params=pltpu.CompilerParams(vmem_limit_bytes=40 * 2**20),
        cost_estimate=pl.CostEstimate(
            flops=units * GROUP * rows * rows * 10 * PAIR,
            bytes_accessed=4 * n * rows * PAIR * heads,
            transcendentals=units * GROUP * rows * rows,
        ),
        name="attend_backward",
    )(place, kv, q_turned, do_turned, q_flat, do_flat, stats)


MESH = pl.DeviceIdType.MESH
GAIN_ROWS = 16


def torus(n):
    side = {32: 4, 8: 2, 4: 1}[n]
    return side, n // (2 * side)


def coordinates(n):
    sy, sz = torus(n)
    ctx, x = lax.axis_index("ctx"), lax.axis_index("wt")
    return {"x": x, "y": ctx // (2 * sz), "z": (ctx // 2) % sz, "core": ctx % 2}


def device_at(n, here, **moved):
    sy, sz = torus(n)
    at = {**here, **moved}
    return ((at["y"] * sz + at["z"]) * 2 + at["core"], at["x"])


def remote(source, target, send, receive, device):
    return pltpu.make_async_remote_copy(
        src_ref=source, dst_ref=target, send_sem=send, recv_sem=receive, device_id=device, device_id_type=MESH
    )


def greet(devices):
    barrier = pltpu.get_barrier_semaphore()
    for device in devices:
        pl.semaphore_signal(barrier, inc=1, device_id=device, device_id_type=MESH)
    pl.semaphore_wait(barrier, len(devices))


def peers_along(n, here, axis, size):
    return [lax.rem(here[axis] + d, size) for d in range(1, size)]


def reduce_kernel(n, sizes, cuts, first, gate, up, down, gains, out, acc, near, near_gains, *scratch):
    steps, sems = scratch[:-7], scratch[-7:]
    local_sem, near_send, near_recv, send_sem, recv_sem, spread_send, spread_recv = sems
    here = coordinates(n)
    sx, sy, sz = sizes["x"], sizes["y"], sizes["z"]
    partner = device_at(n, here, core=1 - here["core"])
    tall = first.shape[0] // sx
    padded, wide = acc.shape[2], acc.shape[3]
    deep = padded // sz
    per_array = first.shape[1] // wide
    block = down.shape[1] // sx
    greet(
        [partner]
        + [device_at(n, here, **{a: i}) for a in "xyz" for i in peers_along(n, here, a, sizes[a])]
    )

    def pieces(core):
        found = []
        for x in range(sx):
            for part in range(sy):
                array, inner = divmod(part, per_array)
                source = ((first, gate), (up, down))[core][array]
                if source is down:
                    for k in range(wide // block):
                        row = (inner * (wide // block) + k) * tall
                        found.append((source.at[pl.ds(row, tall), pl.ds(x * block, block)], x, part, k * block, block))
                else:
                    found.append((source.at[pl.ds(x * tall, tall), pl.ds(inner * wide, wide)], x, part, 0, wide))
        return found

    for core in range(2):
        @pl.when(here["core"] == core)
        def _():
            for source, x, part, column, width in pieces(1 - core):
                remote(
                    source, near.at[x, part, :, pl.ds(column, width)], near_send.at[0], near_recv.at[0], partner
                ).start()
            for source, x, part, column, width in pieces(core):
                pltpu.make_async_copy(
                    source, acc.at[x, part, pl.ds(0, tall), pl.ds(column, width)], local_sem
                ).start()

    to_partner = remote(gains, near_gains, near_send.at[1], near_recv.at[1], partner)
    to_partner.start()
    pltpu.make_async_copy(near, acc.at[:, :, pl.ds(0, tall), :], local_sem).wait()
    whole = remote(near, near, near_send.at[0], near_recv.at[0], partner)
    whole.wait_recv()
    to_partner.wait_recv()
    acc[:, :, tall:, :] = jnp.zeros((sx, sy, padded - tall, wide), BF16)
    both = gains[...].astype(F32) + near_gains[...].astype(F32)
    acc[:, 0, tall : tall + GAIN_ROWS, : gains.shape[2]] = both.astype(BF16)

    def join(i, carry):
        x, part = i // sy, i % sy
        acc[x, part, :tall] = (acc[x, part, :tall].astype(F32) + near[x, part].astype(F32)).astype(BF16)
        return carry

    lax.fori_loop(0, sx * sy, join, 0)

    orders = ("xyz", "yzx", "zxy")

    def region(third, done, axis, index):
        column, width = cuts[third]
        at = {a: here[a] for a in done}
        if axis is not None:
            at[axis] = index
        pick = lambda a: at[a] if a in at else slice(None)
        rows = pl.ds(pl.multiple_of(at["z"] * deep, deep), deep) if "z" in at else slice(None)
        return acc.at[pick("x"), pick("y"), rows, pl.ds(column, width)]

    def copies(third, step):
        axis = orders[third][step]
        size = sizes[axis]
        buffer = steps[third * 3 + step]
        return [
            remote(
                region(third, orders[third][:step], axis, peer),
                buffer.at[d],
                send_sem.at[third, step, d],
                recv_sem.at[third, step, d],
                device_at(n, here, **{axis: peer}),
            )
            for d, peer in enumerate(peers_along(n, here, axis, size))
        ]

    flights = []
    current = [copies(third, 0) for third in range(3)]
    for third in range(3):
        for copy in current[third]:
            copy.start()
    for step in range(3):
        for third in range(3):
            for copy in current[third]:
                copy.wait_recv()
            flights += current[third]
            buffer = steps[third * 3 + step]
            mine = region(third, orders[third][: step + 1], None, None)
            lead = mine.shape[:-2]
            if current[third]:
                def add(i, carry):
                    at = []
                    for extent in reversed(lead):
                        at.append(i % extent)
                        i = i // extent
                    at = tuple(reversed(at))
                    total = mine[at].astype(F32) if at else mine[...].astype(F32)
                    for d in range(len(current[third])):
                        total += buffer[(d, *at)].astype(F32)
                    if at:
                        mine[at] = total.astype(BF16)
                    else:
                        mine[...] = total.astype(BF16)
                    return carry

                count = 1
                for extent in lead:
                    count *= extent
                if count == 1:
                    add(0, 0)
                else:
                    lax.fori_loop(0, count, add, 0)
            if step < 2:
                current[third] = copies(third, step + 1)
                for copy in current[third]:
                    copy.start()

    rows = pl.ds(pl.multiple_of(here["z"] * deep, deep), deep)
    out[here["core"], here["y"], rows, :] = acc[here["x"], here["y"], rows, :]
    half = wide // 2

    def spread(step, part):
        columns = pl.ds(part * half, half)
        axis = "yz"[(step + part) % 2]
        if step == 0:
            piece = out.at[here["core"], here["y"], rows, columns]
        elif axis == "z":
            piece = out.at[here["core"], :, rows, columns]
        else:
            piece = out.at[here["core"], here["y"], :, columns]
        return [
            remote(
                piece, piece, spread_send.at[step, part, d], spread_recv.at[step, part, d],
                device_at(n, here, **{axis: peer}),
            )
            for d, peer in enumerate(peers_along(n, here, axis, sizes[axis]))
        ]

    for step in range(2):
        moved = [spread(step, part) for part in range(2)]
        for part in range(2):
            for copy in moved[part]:
                copy.start()
        for part in range(2):
            for copy in moved[part]:
                copy.wait_recv()
            flights += moved[part]
    home = remote(
        out.at[here["core"]], out.at[here["core"]], near_send.at[2], near_recv.at[2], partner
    )
    home.start()
    home.wait_recv()
    for copy in flights + [to_partner, home, whole]:
        copy.wait_send()


def sum_gradients(first, gate, up, down, gains):
    n, sx = lax.axis_size("ctx"), lax.axis_size("wt")
    sy, sz = torus(n)
    sizes = {"x": sx, "y": sy, "z": sz}
    tall = first.shape[0] // sx
    padded = -(-(tall + GAIN_ROWS) // (16 * sz)) * 16 * sz
    wide = 2 * first.shape[1] // sy
    unit = wide // 128
    widths = [unit * 128 // 3 // 128 * 128] * 2
    widths.append(wide - sum(widths))
    cuts = [(sum(widths[:i]), widths[i]) for i in range(3)]
    orders = ("xyz", "yzx", "zxy")
    extents = {"x": sx, "y": sy}
    buffers = []
    for third in range(3):
        for step in range(3):
            done = orders[third][: step + 1]
            shape = [extents[a] for a in "xy" if a not in done]
            shape.append(padded // sz if "z" in done else padded)
            peers = max(sizes[orders[third][step]] - 1, 1)
            buffers.append(pltpu.VMEM((peers, *shape, cuts[third][1]), BF16))
    peers = max(sx, sy, sz)
    anywhere = pl.BlockSpec(memory_space=pl.ANY)
    inside = pl.BlockSpec(memory_space=pltpu.VMEM)
    dma = pltpu.SemaphoreType.DMA
    return pl.pallas_call(
        functools.partial(reduce_kernel, n, sizes, cuts),
        out_shape=jax.ShapeDtypeStruct((2, sy, padded, wide), BF16),
        in_specs=[anywhere] * 4 + [inside],
        out_specs=inside,
        scratch_shapes=[
            pltpu.VMEM((sx, sy, padded, wide), BF16),
            pltpu.VMEM((sx, sy, tall, wide), BF16),
            pltpu.VMEM(gains.shape, BF16),
            *buffers,
            dma,
            dma((3,)),
            dma((3,)),
            dma((3, 3, peers)),
            dma((3, 3, peers)),
            dma((2, 2, peers)),
            dma((2, 2, peers)),
        ],
        compiler_params=pltpu.CompilerParams(
            collective_id=1, has_side_effects=True, vmem_limit_bytes=56 * 2**20
        ),
        name="sum_gradients",
    )(first, gate, up, down, gains)


def mirror_of(n, here):
    sy, sz = torus(n)
    return device_at(n, here, y=sy - 1 - here["y"], z=sz - 1 - here["z"], core=1 - here["core"])


def plane_peers(n, here, sizes):
    return [device_at(n, here, **{a: i}) for a in "yz" for i in peers_along(n, here, a, sizes[a])]


def gather_kernel(n, own, query, blocks, mirrored, local_sem, step_send, step_recv, near_send, near_recv, far_sem):
    here = coordinates(n)
    sy, sz = torus(n)
    sizes = {"y": sy, "z": sz}
    y, z, core = here["y"], here["z"], here["core"]
    partner, mirror = device_at(n, here, core=1 - core), mirror_of(n, here)
    greet([partner, mirror] + plane_peers(n, here, sizes))
    half = own.shape[1] // 2
    part_rows = [pl.ds(part * half, half) for part in range(2)]

    def along(step, part):
        axis = "yz"[(step + part) % 2]
        rows = part_rows[part]
        copies = []
        for d, peer in enumerate(peers_along(n, here, axis, sizes[axis])):
            if step == 0:
                source, target = own.at[:, rows], blocks.at[:, y, z, core, rows]
            else:
                source = blocks.at[:, :, z, core, rows] if axis == "z" else blocks.at[:, y, :, core, rows]
                target = source
            copies.append(
                remote(
                    source, target, step_send.at[step, part, d], step_recv.at[step, part, d],
                    device_at(n, here, **{axis: peer}),
                )
            )
        return copies

    first = [along(0, 0), along(0, 1)]
    for copy in first[0] + first[1]:
        copy.start()
    to_mirror = remote(query, mirrored, far_sem.at[0], far_sem.at[1], mirror)
    keep = pltpu.make_async_copy(own, blocks.at[:, y, z, core], local_sem)
    keep.start()
    keep.wait()
    for copy in first[0] + first[1]:
        copy.wait_recv()
    second = [along(1, 0), along(1, 1)]
    for copy in second[0] + second[1]:
        copy.start()

    def give(slot, region):
        copy = remote(region, region, near_send.at[slot], near_recv.at[slot], partner)
        copy.start()
        return copy

    passed = [
        give(0, blocks.at[:, :, z, core, part_rows[0]]),
        give(1, blocks.at[:, y, :, core, part_rows[1]]),
    ]
    to_mirror.start()
    for d in range(max(sy, sz) - 1):
        if d < len(second[0]):
            second[0][d].wait_recv()
            passed.append(give(2 + 2 * d, blocks.at[:, :, lax.rem(z + sz - 1 - d, sz), core, part_rows[0]]))
        if d < len(second[1]):
            second[1][d].wait_recv()
            passed.append(give(3 + 2 * d, blocks.at[:, lax.rem(y + sy - 1 - d, sy), :, core, part_rows[1]]))
    for copy in passed:
        copy.wait_recv()
    to_mirror.wait_recv()
    for copy in first[0] + first[1] + second[0] + second[1] + passed + [to_mirror]:
        copy.wait_send()


def gather_blocks(own, query):
    n = lax.axis_size("ctx")
    sy, sz = torus(n)
    peers = max(sy, sz, 2) - 1
    heads, rows, pair = own.shape
    dma = pltpu.SemaphoreType.DMA
    anywhere = pl.BlockSpec(memory_space=pl.ANY)
    blocks, mirrored = pl.pallas_call(
        functools.partial(gather_kernel, n),
        out_shape=(
            jax.ShapeDtypeStruct((heads, sy, sz, 2, rows, pair), BF16),
            jax.ShapeDtypeStruct(query.shape, BF16),
        ),
        in_specs=[anywhere, anywhere],
        out_specs=(anywhere, anywhere),
        scratch_shapes=[
            dma, dma((2, 2, peers)), dma((2, 2, peers)), dma((2 + 2 * peers,)), dma((2 + 2 * peers,)), dma((2,)),
        ],
        compiler_params=pltpu.CompilerParams(collective_id=2, has_side_effects=True),
        name="gather_blocks",
    )(own, query)
    return blocks.reshape(heads, n, rows, pair), mirrored


def home_kernel(n, blocks, query, out, mirrored, acc, near, far, local_sem, near_sem, step_send, step_recv, far_sem, *steps):
    here = coordinates(n)
    sy, sz = torus(n)
    sizes = {"y": sy, "z": sz}
    y, z, core = here["y"], here["z"], here["core"]
    partner, mirror = device_at(n, here, core=1 - core), mirror_of(n, here)
    greet([partner, mirror] + plane_peers(n, here, sizes))
    heads, half = acc.shape[0], acc.shape[3] // 2
    swap = remote(blocks.at[:, :, :, 1 - core], near, near_sem.at[0], near_sem.at[1], partner)
    swap.start()
    keep = pltpu.make_async_copy(blocks.at[:, :, :, core], acc, local_sem)
    keep.start()
    to_mirror = remote(query, far, far_sem.at[0], far_sem.at[1], mirror)
    keep.wait()
    swap.wait_recv()
    to_mirror.start()

    def join(i, carry):
        head, a, b = i // (sy * sz), (i // sz) % sy, i % sz
        acc[head, a, b] = (acc[head, a, b].astype(F32) + near[head, a, b].astype(F32)).astype(BF16)
        return carry

    lax.fori_loop(0, heads * sy * sz, join, 0)

    def region(part, done, axis, index):
        at = {a: here[a] for a in done}
        if axis is not None:
            at[axis] = index
        pick = lambda a: at[a] if a in at else slice(None)
        return acc.at[:, pick("y"), pick("z"), pl.ds(part * half, half)]

    orders = ("yz", "zy")
    flights = []
    for step in range(2):
        moved = []
        for part in range(2):
            axis = orders[part][step]
            moved.append(
                [
                    remote(
                        region(part, orders[part][:step], axis, peer),
                        steps[part * 2 + step].at[d],
                        step_send.at[step, part, d],
                        step_recv.at[step, part, d],
                        device_at(n, here, **{axis: peer}),
                    )
                    for d, peer in enumerate(peers_along(n, here, axis, sizes[axis]))
                ]
            )
            for copy in moved[part]:
                copy.start()
        for part in range(2):
            buffer = steps[part * 2 + step]
            for copy in moved[part]:
                copy.wait_recv()
            flights += moved[part]
            mine = region(part, orders[part][: step + 1], None, None)
            inner = mine.shape[1] if step == 0 else 1
            if moved[part]:
                def add(i, carry):
                    at = (i // inner, i % inner) if step == 0 else (i,)
                    total = mine[at].astype(F32)
                    for d in range(len(moved[part])):
                        total += buffer[(d, *at)].astype(F32)
                    mine[at] = total.astype(BF16)
                    return carry

                lax.fori_loop(0, heads * inner, add, 0)
    out[...] = acc[:, y, z]
    to_mirror.wait_recv()
    mirrored[...] = far[...]
    for copy in flights + [swap, to_mirror]:
        copy.wait_send()


def bring_home(blocks, query):
    n = lax.axis_size("ctx")
    sy, sz = torus(n)
    heads, _, rows, pair = blocks.shape
    dma = pltpu.SemaphoreType.DMA
    peers = max(sy, sz, 2) - 1
    extents = {"y": sy, "z": sz}
    buffers = []
    for order in ("yz", "zy"):
        buffers.append(pltpu.VMEM((max(extents[order[0]] - 1, 1), heads, extents[order[1]], rows // 2, pair), BF16))
        buffers.append(pltpu.VMEM((max(extents[order[1]] - 1, 1), heads, rows // 2, pair), BF16))
    anywhere = pl.BlockSpec(memory_space=pl.ANY)
    inside = pl.BlockSpec(memory_space=pltpu.VMEM)
    return pl.pallas_call(
        functools.partial(home_kernel, n),
        out_shape=(
            jax.ShapeDtypeStruct((heads, rows, pair), BF16),
            jax.ShapeDtypeStruct(query.shape, BF16),
        ),
        in_specs=[anywhere, anywhere],
        out_specs=(inside, inside),
        scratch_shapes=[
            pltpu.VMEM((heads, sy, sz, rows, pair), BF16),
            pltpu.VMEM((heads, sy, sz, rows, pair), BF16),
            pltpu.VMEM(query.shape, BF16),
            dma, dma((2,)), dma((2, 2, peers)), dma((2, 2, peers)), dma((2,)),
            *buffers,
        ],
        compiler_params=pltpu.CompilerParams(
            collective_id=3, has_side_effects=True, vmem_limit_bytes=40 * 2**20
        ),
        name="bring_home",
    )(blocks.reshape(heads, sy, sz, 2, rows, pair), query)


def rms_forward(values, gain):
    inverse = lax.rsqrt(jnp.mean(values * values, axis=-1, keepdims=True) + EPSILON)
    normal = values * inverse
    return (normal * gain, normal, inverse)


def rms_backward(upstream, gain, normal, inverse):
    scaled = upstream * gain
    inner = jnp.mean(scaled * normal, axis=-1, keepdims=True)
    return (inverse * (scaled - normal * inner), jnp.sum(upstream * normal, axis=0))


def positions_of(edges, me, rows):
    token = me * rows + jnp.arange(rows, dtype=jnp.int32)
    start = jnp.where(token >= edges[1], edges[1], jnp.where(token >= edges[0], edges[0], 0))
    return token, token - start


def turn(heads, cosine, sine):
    half = HEAD_SIZE // 2
    low, high = heads[:, :half], heads[:, half:]
    return jnp.concatenate([low * cosine - high * sine, high * cosine + low * sine], axis=1)


def turn_back(heads, cosine, sine):
    half = HEAD_SIZE // 2
    low, high = heads[:, :half], heads[:, half:]
    return jnp.concatenate([low * cosine + high * sine, high * cosine - low * sine], axis=1)


def three_parts(values):
    first = lax.reduce_precision(values, 8, 7)
    rest = values - first
    second = lax.reduce_precision(rest, 8, 7)
    third = rest - second
    return [part.astype(BF16) for part in (first, second, third)]


def joined(parts):
    return parts[0].astype(F32) + parts[1].astype(F32) + parts[2].astype(F32)


def gather_weight(shard):
    return lax.all_gather(shard, "wt", axis=0, tiled=True)


def gather_weight_halves(half):
    n = lax.axis_size("ctx")
    along = lax.all_gather(half, "wt", axis=0)
    return lax.all_gather(along, "ctx", axis=0, axis_index_groups=[[i, i + 1] for i in range(0, n, 2)])


def per_device(
    layer_input,
    doc_bounds,
    attn_gain,
    w_query,
    key_weight,
    value_weight,
    w_out,
    mlp_gain,
    w_gate,
    w_up,
    w_down,
    cotangent,
):
    n = lax.axis_size("ctx")
    me = lax.axis_index("ctx")
    rows, width = layer_input.shape[1:]
    queries = QUERY_HEADS * HEAD_SIZE
    keys = KEY_VALUE_HEADS * HEAD_SIZE
    edges = doc_bounds[0]
    place = jnp.concatenate([jnp.full((1,), me, jnp.int32), edges])
    across = [(i, n - 1 - i) for i in range(n)]

    gains = jnp.pad(jnp.stack([attn_gain, mlp_gain], axis=1), ((0, 0), (0, 62)))
    shard_qkv = jnp.concatenate([w_query, key_weight, value_weight, gains], axis=1)
    full_qkv = gather_weight(shard_qkv)
    gain_rows = full_qkv[:, queries + 2 * keys : queries + 2 * keys + 2].T.astype(F32)
    attn_scale, mlp_scale = gain_rows[0], gain_rows[1]
    full_qkv = full_qkv[:, : queries + 2 * keys]

    x = layer_input[0].astype(F32)
    normed, normal_in, inverse_in = rms_forward(x, attn_scale)
    normed = normed.astype(BF16)
    turned = dot_f32(full_qkv, normed, ((0,), (1,)))
    token, position = positions_of(edges, me, rows)
    freqs = 10000.0 ** (-jnp.arange(HEAD_SIZE // 2, dtype=F32) * 2.0 / HEAD_SIZE)
    angles = freqs[:, None] * position.astype(F32)[None, :]
    cosine, sine = jnp.cos(angles), jnp.sin(angles)

    q = turn(turned[:queries].reshape(QUERY_HEADS, HEAD_SIZE, rows), cosine, sine).astype(BF16)
    k = turn(turned[queries : queries + keys].reshape(KEY_VALUE_HEADS, HEAD_SIZE, rows), cosine, sine).astype(BF16)
    v = turned[queries + keys :].reshape(KEY_VALUE_HEADS, HEAD_SIZE, rows).astype(BF16)
    q = q * BF16(HEAD_SIZE**-0.5)
    own_kv = jnp.concatenate([k, v], axis=1).transpose(0, 2, 1)

    kv, mirrored = gather_blocks(own_kv, q)
    q_both = jnp.stack([q, mirrored])
    blank = jnp.zeros_like(q_both)
    q_turned = jnp.concatenate([q_both, blank], axis=2)
    q_flat = q_turned.transpose(0, 1, 3, 2)

    later = token >= edges[1]
    o_part, stat_part = attention_forward(n, place, kv, q_turned)
    sent = jnp.concatenate([o_part[1].astype(BF16)] + three_parts(stat_part[1]), axis=1)
    got = lax.ppermute(sent, "ctx", across)
    other_stat = joined([got[:, HEAD_SIZE + i : HEAD_SIZE + i + 1] for i in range(3)])
    other_stat = jnp.where(later, NEG, other_stat)
    log_total = jnp.logaddexp(stat_part[0], other_stat)
    attended = o_part[0] * jnp.exp(stat_part[0] - log_total) + got[:, :HEAD_SIZE].astype(F32) * jnp.exp(
        other_stat - log_total
    )
    mixed = attended.reshape(queries, rows).astype(BF16)

    full_out = gather_weight(w_out)
    core = me % 2
    both = gather_weight_halves(jnp.where(core == 0, w_gate, w_up)).reshape(2, width, -1)
    full_gate, full_up = both[0], both[1]
    down_rows = w_down.shape[0] // 2
    both = gather_weight_halves(lax.dynamic_slice_in_dim(w_down, core * down_rows, down_rows))
    full_down = both.transpose(1, 0, 2, 3).reshape(-1, width)
    resid = x + dot_f32(mixed, full_out, ((0,), (0,)))
    normed_two, normal_mlp, inverse_mlp = rms_forward(resid, mlp_scale)
    normed_two = normed_two.astype(BF16)
    gate = dot_f32(normed_two, full_gate)
    up = dot_f32(normed_two, full_up)
    sig = jax.nn.sigmoid(gate)
    activated = gate * sig
    hidden = (activated * up).astype(BF16)
    layer_output = (resid + dot_f32(hidden, full_down)).astype(BF16)[None]
    upstream = cotangent[0]
    grad_w_down = dot_f32(upstream, hidden, ((0,), (0,)))
    grad_hidden = dot_f32(upstream, full_down, ((1,), (1,)))
    grad_up_in = (grad_hidden * activated).astype(BF16)
    grad_gate_in = (grad_hidden * up * sig * (1.0 + gate * (1.0 - sig))).astype(BF16)
    grad_w_gate = dot_f32(normed_two, grad_gate_in, ((0,), (0,)))
    grad_w_up = dot_f32(normed_two, grad_up_in, ((0,), (0,)))
    grad_normed_two = dot_f32(grad_gate_in, full_gate, ((1,), (1,))) + dot_f32(
        grad_up_in, full_up, ((1,), (1,))
    )
    grad_resid_mlp, grad_mlp_gain = rms_backward(grad_normed_two, mlp_scale, normal_mlp, inverse_mlp)
    grad_resid = upstream.astype(F32) + grad_resid_mlp
    grad_mixed = grad_resid.astype(BF16)
    grad_w_out = dot_f32(mixed, grad_mixed)
    grad_attended = dot_f32(full_out, grad_mixed, ((1,), (1,))).astype(BF16)
    grad_attended = grad_attended.reshape(QUERY_HEADS, HEAD_SIZE, rows)
    grad_dot = jnp.sum(grad_attended.astype(F32) * attended, axis=1, keepdims=True)

    before = jnp.where(later, BIG, log_total)
    sent = jnp.concatenate([grad_attended] + three_parts(before) + three_parts(grad_dot), axis=1)
    got = lax.ppermute(sent, "ctx", across)
    piece = lambda i: got[:, HEAD_SIZE + i : HEAD_SIZE + i + 1]
    stats = jnp.stack(
        [
            jnp.concatenate([before, grad_dot], axis=1),
            jnp.concatenate([joined([piece(0), piece(1), piece(2)]), joined([piece(3), piece(4), piece(5)])], axis=1),
            jnp.concatenate([log_total, grad_dot], axis=1),
        ]
    )
    do_both = jnp.stack([grad_attended, got[:, :HEAD_SIZE]])
    do_turned = jnp.concatenate([blank, do_both], axis=2)
    do_flat = do_turned.transpose(0, 1, 3, 2)
    dq, dkv = attention_backward(n, place, kv, q_turned, do_turned, q_flat, do_flat, stats)
    dkv, dq_more = bring_home(dkv, dq[1].astype(BF16))
    grad_q = turn_back((dq[0] + dq_more.astype(F32)) * HEAD_SIZE**-0.5, cosine, sine).astype(BF16)
    dkv = dkv.astype(F32).transpose(0, 2, 1)
    grad_k = turn_back(dkv[:, :HEAD_SIZE], cosine, sine).astype(BF16)
    grad_v = dkv[:, HEAD_SIZE:].astype(BF16)
    grad_qkv = jnp.concatenate(
        [grad_q.reshape(queries, rows), grad_k.reshape(keys, rows), grad_v.reshape(keys, rows)]
    )
    grad_w_qkv = dot_f32(normed, grad_qkv, ((0,), (1,)))
    grad_normed = dot_f32(grad_qkv, full_qkv, ((0,), (1,)))
    grad_in, grad_attn_gain = rms_backward(grad_normed, attn_scale, normal_in, inverse_in)
    input_grad = (grad_resid + grad_in)[None]

    sx = lax.axis_size("wt")
    tall = width // sx
    gains = jnp.stack([grad_attn_gain, grad_mlp_gain]).reshape(2, sx, tall).transpose(1, 0, 2)
    gains = jnp.pad(gains, ((0, 0), (0, GAIN_ROWS - 2), (0, -tall % 128))).astype(BF16)
    first = jnp.concatenate([grad_w_qkv.astype(BF16), grad_w_out.astype(BF16)], axis=1)
    sums = sum_gradients(
        first, grad_w_gate.astype(BF16), grad_w_up.astype(BF16), grad_w_down.astype(BF16), gains
    )
    parts = sums.reshape(-1, *sums.shape[2:])
    parts = jnp.concatenate([parts[i] for i in range(parts.shape[0])], axis=1)
    gain_sums = parts[tall : tall + 2, :tall].astype(F32)
    parts = parts[:tall].astype(F32)
    ff = w_gate.shape[1]
    block = ff // sx
    sum_down = jnp.concatenate([parts[:, 3 * ff + i * block : 3 * ff + (i + 1) * block] for i in range(sx)]).T
    return (
        layer_output,
        input_grad,
        gain_sums[0],
        parts[:, :queries],
        parts[:, queries : queries + keys],
        parts[:, queries + keys : queries + 2 * keys],
        parts[:, queries + 2 * keys : ff],
        gain_sums[1],
        parts[:, ff : 2 * ff],
        parts[:, 2 * ff : 3 * ff],
        sum_down,
    )


def solution(mesh):
    tokens, weights, gains = P("wt", "ctx", None), P("wt", None), P("wt")
    return jax.shard_map(
        per_device,
        mesh=mesh,
        in_specs=(
            tokens, weights, gains, weights, weights, weights, weights, gains, weights, weights, weights, tokens,
        ),
        out_specs=(
            tokens, tokens, gains, weights, weights, weights, weights, gains, weights, weights, weights,
        ),
        check_vma=False,
    )
```

```python
import functools

import jax
import jax.numpy as jnp
from jax import lax
from jax.experimental import pallas as pl
from jax.experimental.pallas import tpu as pltpu
from jax.sharding import PartitionSpec as P

QUERY_HEADS = 15
KEY_VALUE_HEADS = 5
HEAD_SIZE = 64
GROUP = QUERY_HEADS // KEY_VALUE_HEADS
PAIR = 2 * HEAD_SIZE
EPSILON = 1e-05
NEG = -1e30
BIG = 1e30
TAIL = 16
LOG2E = 1.4426950408889634
F32 = jnp.float32
BF16 = jnp.bfloat16


def dot_f32(left, right, dims=((1,), (0,))):
    return lax.dot_general(left, right, (dims, ((), ())), preferred_element_type=F32)


def ranges(me, half):
    light = me < half
    first = jnp.where(light, 0, me - half + 1)
    mirrored = jnp.where(light, half - me, 0)
    return first, mirrored


def query_index(owner, rows, height):
    column = lax.broadcasted_iota(jnp.int32, (height, GROUP * rows), 1)
    return owner * rows + (column & (rows - 1))


def visible_pairs(b0, b1, block, owner, rows):
    key = block * rows + lax.broadcasted_iota(jnp.int32, (rows, GROUP * rows), 0)
    query = query_index(owner, rows, rows)
    return (key <= query) & ((key >= b0) | (query < b0)) & ((key >= b1) | (query < b1))


def sweep(me, n, widest, step):
    first, mirrored = ranges(me, n // 2)

    def plain(which, low, high):
        turns = (high - low) // widest

        def several(i, carry):
            step(which, low + i * widest, widest, False, False)
            return carry

        lax.fori_loop(0, turns, several, 0)
        at, count = low + turns * widest, widest // 2
        while count:
            more = (high - at) >= count

            def rest(at=at, count=count):
                step(which, at, count, False, False)

            pl.when(more)(rest)
            at = at + jnp.where(more, count, 0)
            count //= 2

    @pl.when((first == 0) & (me > 0))
    def _():
        step(0, 0, 1, True, False)

    low = jnp.maximum(first, 1)
    plain(0, low, jnp.maximum(me, low))
    step(0, me, 1, True, True)

    @pl.when(mirrored > 0)
    def _():
        step(1, 0, 1, True, False)
        plain(1, 1, mirrored)


def lay_out(wide, first_row, own, mirrored):
    rows = own.shape[-1]
    for which, source in enumerate((own, mirrored)):
        wide[which] = jnp.zeros(wide.shape[1:], BF16)
        for g in range(GROUP):
            wide[which, first_row : first_row + HEAD_SIZE, g * rows : (g + 1) * rows] = source[g, :HEAD_SIZE]


def split_three(values):
    first = values.astype(BF16)
    rest = values - first.astype(F32)
    second = rest.astype(BF16)
    third = (rest - second.astype(F32)).astype(BF16)
    return first, second, third


def forward_kernel(n, place, kv_ref, q_own, q_mirrored, o_ref, stat_ref, sent_ref, wide_q, peak, mass, total):
    me, b0, b1 = place[0], place[1], place[2]
    rows = q_own.shape[-1]
    peak[...] = jnp.full_like(peak, NEG)
    mass[...] = jnp.zeros_like(mass)
    total[...] = jnp.zeros_like(total)
    lay_out(wide_q, 0, q_own, q_mirrored)

    def step(which, block, count, masked, diagonal):
        kv = kv_ref[pl.ds(pl.multiple_of(block * rows, rows), count * rows)]
        v_turned = kv.T[HEAD_SIZE:]
        old, held, summed = peak[which], mass[which], total[which]
        if diagonal:
            fresh = query_index(me, rows, 1) >= b1
            old = jnp.where(fresh, NEG, old)
            held = jnp.where(fresh, 0.0, held)
            summed = jnp.where(fresh, 0.0, summed)
        scores = dot_f32(kv, wide_q[which])
        if masked:
            owner = me if which == 0 else n - 1 - me
            scores = jnp.where(visible_pairs(b0, b1, block, owner, rows), scores, NEG)
        new = jnp.maximum(old, jnp.max(scores, axis=0, keepdims=True))
        weights = jnp.exp2((scores - new) * LOG2E)
        factor = jnp.exp2((old - new) * LOG2E)
        peak[which] = new
        mass[which] = held * factor + jnp.sum(weights, axis=0, keepdims=True)
        total[which] = summed * factor + dot_f32(v_turned, weights.astype(BF16))

    sweep(me, n, 4, step)
    for which in range(2):
        held = mass[which]
        live = held > 0.0
        safe = jnp.where(live, held, 1.0)
        result = total[which] / safe
        stat = jnp.where(live, peak[which] + jnp.log(safe), NEG)
        for g in range(GROUP):
            columns = slice(g * rows, (g + 1) * rows)
            if which == 0:
                o_ref[g] = result[:, columns]
                stat_ref[g] = stat[:, columns]
            else:
                sent_ref[g, :HEAD_SIZE] = result[:, columns].astype(BF16)
                tail = [part.astype(F32) for part in split_three(stat[:, columns])]
                tail.append(jnp.zeros((TAIL - 3, rows), F32))
                sent_ref[g, HEAD_SIZE:] = jnp.concatenate(tail).astype(BF16)


def per_group(*shape):
    return pl.BlockSpec((GROUP, *shape), lambda j: (j,) + (0,) * len(shape))


def attention_forward(n, place, kv, q_own, q_mirrored):
    heads, rows = kv.shape[0], q_own.shape[-1]
    units = (n + 1) * heads
    columns = GROUP * rows
    return pl.pallas_call(
        functools.partial(forward_kernel, n),
        grid=(heads,),
        out_shape=(
            jax.ShapeDtypeStruct((QUERY_HEADS, HEAD_SIZE, rows), F32),
            jax.ShapeDtypeStruct((QUERY_HEADS, 1, rows), F32),
            jax.ShapeDtypeStruct((QUERY_HEADS, HEAD_SIZE + TAIL, rows), BF16),
        ),
        in_specs=[
            pl.BlockSpec(memory_space=pltpu.SMEM),
            pl.BlockSpec((None, n * rows, PAIR), lambda j: (j, 0, 0)),
            per_group(HEAD_SIZE, rows),
            per_group(HEAD_SIZE, rows),
        ],
        out_specs=(per_group(HEAD_SIZE, rows), per_group(1, rows), per_group(HEAD_SIZE + TAIL, rows)),
        scratch_shapes=[
            pltpu.VMEM((2, PAIR, columns), BF16),
            pltpu.VMEM((2, 1, columns), F32),
            pltpu.VMEM((2, 1, columns), F32),
            pltpu.VMEM((2, HEAD_SIZE, columns), F32),
        ],
        compiler_params=pltpu.CompilerParams(vmem_limit_bytes=40 * 2**20),
        cost_estimate=pl.CostEstimate(
            flops=units * GROUP * rows * rows * 24 * PAIR,
            bytes_accessed=2 * n * rows * PAIR * heads,
            transcendentals=units * GROUP * rows * rows,
        ),
        name="attend_forward",
    )(place, kv, q_own, q_mirrored)


MESH = pl.DeviceIdType.MESH
GAIN_ROWS = 16


def torus(n):
    side = {32: 4, 8: 2, 4: 1}[n]
    return side, n // (2 * side)


def coordinates(n):
    sy, sz = torus(n)
    ctx, x = lax.axis_index("ctx"), lax.axis_index("wt")
    return {"x": x, "y": ctx // (2 * sz), "z": (ctx // 2) % sz, "core": ctx % 2}


def device_at(n, here, **moved):
    sy, sz = torus(n)
    at = {**here, **moved}
    return ((at["y"] * sz + at["z"]) * 2 + at["core"], at["x"])


def remote(source, target, send, receive, device):
    return pltpu.make_async_remote_copy(
        src_ref=source, dst_ref=target, send_sem=send, recv_sem=receive, device_id=device, device_id_type=MESH
    )


def greet(devices):
    barrier = pltpu.get_barrier_semaphore()
    for device in devices:
        pl.semaphore_signal(barrier, inc=1, device_id=device, device_id_type=MESH)
    pl.semaphore_wait(barrier, len(devices))


def peers_along(n, here, axis, size):
    return [lax.rem(here[axis] + d, size) for d in range(1, size)]


def mirror_of(n, here):
    sy, sz = torus(n)
    return device_at(n, here, y=sy - 1 - here["y"], z=sz - 1 - here["z"], core=1 - here["core"])


def plane_peers(n, here, sizes):
    return [device_at(n, here, **{a: i}) for a in "yz" for i in peers_along(n, here, a, sizes[a])]


def gather_kernel(n, own, query, blocks, mirrored, local_sem, step_send, step_recv, near_send, near_recv, far_sem):
    here = coordinates(n)
    sy, sz = torus(n)
    sizes = {"y": sy, "z": sz}
    y, z, core = here["y"], here["z"], here["core"]
    partner, mirror = device_at(n, here, core=1 - core), mirror_of(n, here)
    greet([partner, mirror] + plane_peers(n, here, sizes))
    half = own.shape[1] // 2
    part_rows = [pl.ds(part * half, half) for part in range(2)]

    def along(step, part):
        axis = "yz"[(step + part) % 2]
        rows = part_rows[part]
        copies = []
        for d, peer in enumerate(peers_along(n, here, axis, sizes[axis])):
            if step == 0:
                source, target = own.at[:, rows], blocks.at[:, y, z, core, rows]
            else:
                source = blocks.at[:, :, z, core, rows] if axis == "z" else blocks.at[:, y, :, core, rows]
                target = source
            copies.append(
                remote(
                    source, target, step_send.at[step, part, d], step_recv.at[step, part, d],
                    device_at(n, here, **{axis: peer}),
                )
            )
        return copies

    first = [along(0, 0), along(0, 1)]
    for copy in first[0] + first[1]:
        copy.start()
    to_mirror = remote(query, mirrored, far_sem.at[0], far_sem.at[1], mirror)
    keep = pltpu.make_async_copy(own, blocks.at[:, y, z, core], local_sem)
    keep.start()
    keep.wait()
    for copy in first[0] + first[1]:
        copy.wait_recv()
    second = [along(1, 0), along(1, 1)]
    for copy in second[0] + second[1]:
        copy.start()

    def give(slot, region):
        copy = remote(region, region, near_send.at[slot], near_recv.at[slot], partner)
        copy.start()
        return copy

    passed = [
        give(0, blocks.at[:, :, z, core, part_rows[0]]),
        give(1, blocks.at[:, y, :, core, part_rows[1]]),
    ]
    to_mirror.start()
    for d in range(max(sy, sz) - 1):
        if d < len(second[0]):
            second[0][d].wait_recv()
            passed.append(give(2 + 2 * d, blocks.at[:, :, lax.rem(z + sz - 1 - d, sz), core, part_rows[0]]))
        if d < len(second[1]):
            second[1][d].wait_recv()
            passed.append(give(3 + 2 * d, blocks.at[:, lax.rem(y + sy - 1 - d, sy), :, core, part_rows[1]]))
    for copy in passed:
        copy.wait_recv()
    to_mirror.wait_recv()
    for copy in first[0] + first[1] + second[0] + second[1] + passed + [to_mirror]:
        copy.wait_send()


def gather_blocks(own, query):
    n = lax.axis_size("ctx")
    sy, sz = torus(n)
    peers = max(sy, sz, 2) - 1
    heads, rows, pair = own.shape
    dma = pltpu.SemaphoreType.DMA
    anywhere = pl.BlockSpec(memory_space=pl.ANY)
    blocks, mirrored = pl.pallas_call(
        functools.partial(gather_kernel, n),
        out_shape=(
            jax.ShapeDtypeStruct((heads, sy, sz, 2, rows, pair), BF16),
            jax.ShapeDtypeStruct(query.shape, BF16),
        ),
        in_specs=[anywhere, anywhere],
        out_specs=(anywhere, anywhere),
        scratch_shapes=[
            dma, dma((2, 2, peers)), dma((2, 2, peers)), dma((2 + 2 * peers,)), dma((2 + 2 * peers,)), dma((2,)),
        ],
        compiler_params=pltpu.CompilerParams(collective_id=2, has_side_effects=True),
        cost_estimate=pl.CostEstimate(flops=5 * 10**10, bytes_accessed=heads * n * rows * pair * 4, transcendentals=0),
        name="gather_blocks",
    )(own, query)
    return blocks, mirrored


def exchange_kernel(n, sent, wide, down, got, full_wide, full_down, local_sem, send_sem, recv_sem):
    here = coordinates(n)
    core = here["core"]
    partner, mirror = device_at(n, here, core=1 - core), mirror_of(n, here)
    greet([partner, mirror])
    mine = [full_wide.at[core], full_down.at[:, core]]
    copies = [
        remote(source, target, send_sem.at[i], recv_sem.at[i], device)
        for i, (source, target, device) in enumerate(
            [(sent, got, mirror), (wide, mine[0], partner), (down, mine[1], partner)]
        )
    ]
    copies += [pltpu.make_async_copy(source, mine[i], local_sem.at[i]) for i, source in enumerate((wide, down))]
    for copy in copies:
        copy.start()
    for copy in copies:
        copy.wait()


def exchange(sent, wide, down):
    n = lax.axis_size("ctx")
    anywhere = pl.BlockSpec(memory_space=pl.ANY)
    dma = pltpu.SemaphoreType.DMA
    sx, rows, columns = down.shape
    return pl.pallas_call(
        functools.partial(exchange_kernel, n),
        out_shape=(
            jax.ShapeDtypeStruct(sent.shape, BF16),
            jax.ShapeDtypeStruct((2, *wide.shape), BF16),
            jax.ShapeDtypeStruct((sx, 2, rows, columns), BF16),
        ),
        in_specs=[anywhere] * 3,
        out_specs=(anywhere,) * 3,
        scratch_shapes=[dma((2,)), dma((3,)), dma((3,))],
        compiler_params=pltpu.CompilerParams(collective_id=4, has_side_effects=True),
        cost_estimate=pl.CostEstimate(flops=10**10, bytes_accessed=4 * wide.size, transcendentals=0),
        name="exchange",
    )(sent, wide, down)


ORDERS = ("xyz", "yzx", "zxy")


class TreeSum:
    def __init__(self, n, sizes, cuts, acc, near, steps, local_sem, near_send, near_recv, send_sem, recv_sem):
        self.n, self.sizes, self.cuts, self.acc, self.near, self.steps = n, sizes, cuts, acc, near, steps
        self.local_sem, self.near_send, self.near_recv = local_sem, near_send, near_recv
        self.send_sem, self.recv_sem = send_sem, recv_sem
        self.here = coordinates(n)
        self.partner = device_at(n, self.here, core=1 - self.here["core"])

    def place(self, buffer, x, chunk, column, width):
        deep, sz = buffer.shape[3], buffer.shape[2]
        row = chunk * 16
        inner = 0 if deep == 16 else pl.multiple_of(row % deep, 16)
        return buffer.at[x, row // (deep * sz), (row // deep) % sz, pl.ds(inner, 16), pl.ds(column, width)]

    def swap(self, pieces, tall):
        chunks, sx = tall // 16, self.sizes["x"]
        for core in range(2):

            def send(core=core):
                def one(i, carry):
                    x, chunk = i // chunks, i % chunks
                    for slot, (source, column, width) in enumerate(pieces(1 - core)):
                        remote(
                            source(x, chunk), self.place(self.near, x, chunk, column, width),
                            self.near_send.at[slot], self.near_recv.at[slot], self.partner,
                        ).start()
                    for slot, (source, column, width) in enumerate(pieces(core)):
                        pltpu.make_async_copy(
                            source(x, chunk), self.place(self.acc, x, chunk, column, width), self.local_sem.at[slot]
                        ).start()
                    return carry

                lax.fori_loop(0, sx * chunks, one, 0)

            pl.when(self.here["core"] == core)(send)

    def join(self, wholes, tall):
        for slot, whole in enumerate(wholes):
            pltpu.make_async_copy(whole, whole, self.local_sem.at[slot]).wait()
            remote(whole, whole, self.near_send.at[slot], self.near_recv.at[slot], self.partner).wait_recv()
        acc, near = self.acc, self.near
        sx, sy, sz, deep, wide = acc.shape
        chunks, every = tall // 16, sy * sz * deep // 16

        def one(i, carry):
            x, chunk = i // chunks, i % chunks
            mine = self.place(acc, x, chunk, 0, wide)
            mine[...] = mine[...] + self.place(near, x, chunk, 0, wide)[...]
            return carry

        lax.fori_loop(0, sx * chunks, one, 0)
        spare = every - chunks

        def blank(i, carry):
            target = self.place(acc, i // spare, chunks + i % spare, 0, wide)
            target[...] = jnp.zeros((16, wide), BF16)
            return carry

        lax.fori_loop(0, sx * spare, blank, 0)

    def sent_swap(self, wholes):
        for slot, whole in enumerate(wholes):
            remote(whole, whole, self.near_send.at[slot], self.near_recv.at[slot], self.partner).wait_send()

    def region(self, third, done, axis=None, index=None):
        column, width = self.cuts[third]
        at = {a: self.here[a] for a in done}
        if axis is not None:
            at[axis] = index
        pick = [at[a] if a in at else slice(None) for a in "xyz"]
        return self.acc.at[(*pick, slice(None), pl.ds(column, width))]

    def copies(self, third, step):
        axis = ORDERS[third][step]
        return [
            remote(
                self.region(third, ORDERS[third][:step], axis, peer),
                self.steps[third * 3 + step].at[d],
                self.send_sem.at[third, step, d],
                self.recv_sem.at[third, step, d],
                device_at(self.n, self.here, **{axis: peer}),
            )
            for d, peer in enumerate(peers_along(self.n, self.here, axis, self.sizes[axis]))
        ]

    def start(self, step):
        for third in range(3):
            for copy in self.copies(third, step):
                copy.start()

    def finish(self, step, follow):
        for third in range(3):
            copies = self.copies(third, step)
            for copy in copies:
                copy.wait_recv()
            buffer = self.steps[third * 3 + step]
            mine = self.region(third, ORDERS[third][: step + 1])
            lead = mine.shape[:-2]
            count = 1
            for extent in lead:
                count *= extent

            def add(i, carry):
                at = []
                for extent in reversed(lead):
                    at.append(i % extent)
                    i = i // extent
                at = tuple(reversed(at))
                total = mine[(*at, slice(None), slice(None))].astype(F32)
                for d in range(len(copies)):
                    total += buffer[(d, *at)].astype(F32)
                mine[(*at, slice(None), slice(None))] = total.astype(BF16)
                return carry

            if count == 1:
                add(0, 0)
            else:
                lax.fori_loop(0, count, add, 0)
            if follow:
                for copy in self.copies(third, step + 1):
                    copy.start()

    def sent_steps(self):
        for step in range(3):
            for third in range(3):
                for copy in self.copies(third, step):
                    copy.wait_send()


def tree_peers(n, here, sizes):
    return [device_at(n, here, **{a: i}) for a in "xyz" for i in peers_along(n, here, a, sizes[a])]


def tree_layout(n, sx, tall, wide):
    sy, sz = torus(n)
    sizes = {"x": sx, "y": sy, "z": sz}
    deep = -(-(tall + GAIN_ROWS) // (16 * sy * sz)) * 16
    third = wide // 384 * 128
    cuts = [(0, third), (third, third), (2 * third, wide - 2 * third)]
    buffers = []
    for order, (_, width) in zip(ORDERS, cuts):
        for step in range(3):
            shape = [sizes[a] for a in "xyz" if a not in order[: step + 1]]
            buffers.append(pltpu.VMEM((max(sizes[order[step]] - 1, 1), *shape, deep, width), BF16))
    peers = max(sx, sy, sz)
    dma = pltpu.SemaphoreType.DMA
    sems = [dma((2,)), dma((2,)), dma((2,)), dma((3, 3, peers)), dma((3, 3, peers))]
    block = pltpu.VMEM((sx, sy, sz, deep, wide), BF16)
    return sizes, cuts, [block, block], buffers, sems


def backward_kernel(
    n, sizes, cuts, tall, place, kv_ref, q_own, q_mirrored, do_own, do_mirrored, stat_ref, gate, up, down,
    dq_ref, home_ref, piece_ref,
    wide_q, wide_do, tall_q, tall_do, stats, dq, gathered, dq_stage, dq_far, kv_acc, kv_near, kv_stage, *rest,
):
    kv_steps, rest = rest[:4], rest[4:]
    swap_send, swap_recv, step_send, step_recv, far_send, far_recv = rest[:6]
    rest = rest[6:]
    tree = TreeSum(n, sizes, cuts, rest[0], rest[1], rest[2:11], *rest[11:])
    here = coordinates(n)
    sy, sz = torus(n)
    y, z, core = here["y"], here["z"], here["core"]
    partner, mirror = tree.partner, mirror_of(n, here)
    me, b0, b1 = lax.axis_index("ctx"), place[1], place[2]
    head = pl.program_id(0)
    heads = home_ref.shape[0]
    rows = q_own.shape[-1]
    half = n // 2
    first, _ = ranges(me, half)
    width = gate.shape[1]
    block = width // sizes["x"]

    def pieces(of):
        main = (gate, up)[of]
        found = [(lambda x, c: main.at[pl.ds(pl.multiple_of(x * tall + c * 16, 16), 16), :], 0, width)]
        each = sizes["x"] // 2
        for k in range(each):
            row = (of * each + k) * tall
            found.append(
                (
                    lambda x, c, row=row: down.at[
                        pl.ds(pl.multiple_of(row + c * 16, 16), 16), pl.ds(pl.multiple_of(x * block, 128), block)
                    ],
                    width + k * block,
                    block,
                )
            )
        return found

    wholes = [gate] + [down.at[pl.ds(0, tall), :]] * (sizes["x"] // 2)

    def swap(h):
        return remote(kv_stage.at[h % 2], kv_near.at[h], swap_send.at[h], swap_recv.at[h], partner)

    def region(h, part, done, axis=None, index=None):
        at = {a: here[a] for a in done}
        if axis is not None:
            at[axis] = index
        pick = [at[a] if a in at else slice(None) for a in "yz"]
        return kv_acc.at[(h, *pick, pl.ds(part * (rows // 2), rows // 2))]

    def steps(h, step, part):
        order = ("yz", "zy")[part]
        axis = order[step]
        return [
            remote(
                region(h, part, order[:step], axis, peer),
                kv_steps[part * 2 + step].at[h, d],
                step_send.at[h, step * 2 + part, d],
                step_recv.at[h, step * 2 + part, d],
                device_at(n, here, **{axis: peer}),
            )
            for d, peer in enumerate(peers_along(n, here, axis, sizes[axis]))
        ]

    def start_steps(h, step):
        for part in range(2):
            for copy in steps(h, step, part):
                copy.start()

    def finish_swap(h):
        swap(h).wait_recv()

        def one(i, carry):
            a, b = i // sz, i % sz
            kv_acc[h, a, b] = kv_acc[h, a, b] + kv_near[h, a, b]
            return carry

        lax.fori_loop(0, sy * sz, one, 0)
        start_steps(h, 0)

    def finish_step(h, step):
        for part in range(2):
            copies = steps(h, step, part)
            for copy in copies:
                copy.wait_recv()
            buffer = kv_steps[part * 2 + step]
            mine = region(h, part, ("yz", "zy")[part][: step + 1])
            for i in range(mine.shape[0] if step == 0 else 1):
                at = (i,) if step == 0 else ()
                total = mine[(*at, slice(None), slice(None))].astype(F32)
                for d in range(len(copies)):
                    total += buffer[(h, d, *at)].astype(F32)
                mine[(*at, slice(None), slice(None))] = total.astype(BF16)
        if step == 0:
            start_steps(h, 1)
        else:
            home_ref[h] = kv_acc[h, y, z]

    def to_mirror(h):
        return remote(dq_stage.at[h], dq_far.at[h], far_send.at[h], far_recv.at[h], mirror)

    @pl.when(head == 0)
    def _():
        greet([partner, mirror] + tree_peers(n, here, sizes))
        tree.swap(pieces, tall)

    gathered[...] = jnp.zeros_like(gathered)
    dq[...] = jnp.zeros_like(dq)
    lay_out(wide_q, 0, q_own, q_mirrored)
    lay_out(wide_do, HEAD_SIZE, do_own, do_mirrored)
    for which in range(2):
        for g in range(GROUP):
            columns = slice(g * rows, (g + 1) * rows)
            tall_q[which, columns] = wide_q[which, :, columns].T
            tall_do[which, columns] = wide_do[which, :, columns].T
    for g in range(GROUP):
        columns = slice(g * rows, (g + 1) * rows)
        got = do_mirrored[g, HEAD_SIZE:].astype(F32)
        stats[0, :, columns] = jnp.concatenate([stat_ref[g, 0:1], stat_ref[g, 2:3]])
        stats[1, :, columns] = jnp.concatenate([got[0:1] + got[1:2] + got[2:3], got[3:4] + got[4:5] + got[5:6]])
        stats[2, :, columns] = stat_ref[g, 1:3]

    def attend(which, block, count, masked, diagonal):
        kv = kv_ref[pl.ds(pl.multiple_of(block * rows, rows), count * rows)]
        k_turned = kv.T[:HEAD_SIZE]
        kind = 2 if diagonal else which
        scores = dot_f32(kv, wide_q[which])
        weights = jnp.exp2((scores - stats[kind, 0:1]) * LOG2E)
        if masked:
            owner = me if which == 0 else n - 1 - me
            weights = jnp.where(visible_pairs(b0, b1, block, owner, rows), weights, 0.0)
        weight_grad = dot_f32(kv, wide_do[which])
        score_grad = (weights * (weight_grad - stats[kind, 1:2])).astype(BF16)
        more = dot_f32(score_grad, tall_q[which]) + dot_f32(weights.astype(BF16), tall_do[which])
        dq[which] += dot_f32(k_turned, score_grad)
        at = pl.ds(pl.multiple_of((block - first) * rows, rows), count * rows)
        gathered[at] += more

    sweep(me, n, 2, attend)

    for g in range(GROUP):
        columns = slice(g * rows, (g + 1) * rows)
        dq_ref[head * GROUP + g] = dq[0, :, columns]
        dq_stage[head, g] = dq[1, :, columns].astype(BF16)
    to_mirror(head).start()

    @pl.when(head >= 2)
    def _():
        swap(head - 2).wait_send()

    def take(i, carry):
        a, b = i // sz, i % sz
        for target, which_core in ((kv_acc.at[head, a, b], core), (kv_stage.at[head % 2, a, b], 1 - core)):
            slot = 2 * i + which_core - first
            inside = (slot >= 0) & (slot < half)
            at = jnp.clip(slot, 0, half - 1)
            values = gathered[pl.ds(pl.multiple_of(at * rows, rows), rows)]
            target[...] = jnp.where(inside, values, 0.0).astype(BF16)
        return carry

    lax.fori_loop(0, sy * sz, take, 0)
    swap(head).start()

    @pl.when(head >= 1)
    def _():
        finish_swap(head - 1)

    @pl.when(head >= 2)
    def _():
        finish_step(head - 2, 0)

    @pl.when(head >= 3)
    def _():
        finish_step(head - 3, 1)

    @pl.when(head == 0)
    def _():
        tree.join(wholes, tall)
        tree.start(0)

    @pl.when(head == 3)
    def _():
        tree.finish(0, True)

    @pl.when(head == heads - 1)
    def _():
        last = heads - 1
        finish_swap(last)
        finish_step(last - 1, 0)
        tree.finish(1, True)
        finish_step(last - 2, 1)
        tree.finish(2, False)
        piece_ref[...] = tree.acc[here["x"], y, z]
        finish_step(last, 0)
        finish_step(last - 1, 1)
        for h in range(heads):
            to_mirror(h).wait_recv()
            for g in range(GROUP):
                dq_ref[h * GROUP + g] += dq_far[h, g].astype(F32)
        finish_step(last, 1)
        for h in range(heads):
            to_mirror(h).wait_send()
            for step in range(2):
                for part in range(2):
                    for copy in steps(h, step, part):
                        copy.wait_send()
        swap(last - 1).wait_send()
        swap(last).wait_send()
        tree.sent_swap(wholes)
        tree.sent_steps()


def attention_backward(n, place, kv, q_own, q_mirrored, do_own, do_mirrored, stats, gate, up, down):
    heads, rows = kv.shape[0], q_own.shape[-1]
    units = (n + 1) * heads
    columns = GROUP * rows
    sx = lax.axis_size("wt")
    sy, sz = torus(n)
    tall = gate.shape[0] // sx
    wide = gate.shape[1] + gate.shape[1] // 2
    sizes, cuts, blocks, buffers, sems = tree_layout(n, sx, tall, wide)
    sems[0:3] = [pltpu.SemaphoreType.DMA((1 + sx // 2,))] * 3
    extents = {"y": sy, "z": sz}
    kv_steps = []
    for order in ("yz", "zy"):
        kv_steps.append(
            pltpu.VMEM((heads, max(extents[order[0]] - 1, 1), extents[order[1]], rows // 2, PAIR), BF16)
        )
        kv_steps.append(pltpu.VMEM((heads, max(extents[order[1]] - 1, 1), rows // 2, PAIR), BF16))
    peers = max(sy, sz, 2) - 1
    dma = pltpu.SemaphoreType.DMA
    anywhere = pl.BlockSpec(memory_space=pl.ANY)
    fixed = lambda *shape: pl.BlockSpec(shape, lambda j: (0,) * len(shape))
    deep = blocks[0].shape[3]
    return pl.pallas_call(
        functools.partial(backward_kernel, n, sizes, cuts, tall),
        grid=(heads,),
        out_shape=(
            jax.ShapeDtypeStruct((QUERY_HEADS, HEAD_SIZE, rows), F32),
            jax.ShapeDtypeStruct((heads, rows, PAIR), BF16),
            jax.ShapeDtypeStruct((deep, wide), BF16),
        ),
        in_specs=[
            pl.BlockSpec(memory_space=pltpu.SMEM),
            pl.BlockSpec((None, n * rows, PAIR), lambda j: (j, 0, 0)),
            per_group(HEAD_SIZE, rows),
            per_group(HEAD_SIZE, rows),
            per_group(HEAD_SIZE, rows),
            per_group(HEAD_SIZE + TAIL, rows),
            per_group(3, rows),
            anywhere,
            anywhere,
            anywhere,
        ],
        out_specs=(fixed(QUERY_HEADS, HEAD_SIZE, rows), fixed(heads, rows, PAIR), fixed(deep, wide)),
        scratch_shapes=[
            pltpu.VMEM((2, PAIR, columns), BF16),
            pltpu.VMEM((2, PAIR, columns), BF16),
            pltpu.VMEM((2, columns, PAIR), BF16),
            pltpu.VMEM((2, columns, PAIR), BF16),
            pltpu.VMEM((3, 2, columns), F32),
            pltpu.VMEM((2, HEAD_SIZE, columns), F32),
            pltpu.VMEM((n // 2 * rows, PAIR), F32),
            pltpu.VMEM((heads, GROUP, HEAD_SIZE, rows), BF16),
            pltpu.VMEM((heads, GROUP, HEAD_SIZE, rows), BF16),
            pltpu.VMEM((heads, sy, sz, rows, PAIR), BF16),
            pltpu.VMEM((heads, sy, sz, rows, PAIR), BF16),
            pltpu.VMEM((2, sy, sz, rows, PAIR), BF16),
            *kv_steps,
            dma((heads,)), dma((heads,)), dma((heads, 4, peers)), dma((heads, 4, peers)), dma((heads,)), dma((heads,)),
            *blocks,
            *buffers,
            *sems,
        ],
        compiler_params=pltpu.CompilerParams(
            collective_id=3, has_side_effects=True, vmem_limit_bytes=61 * 2**20
        ),
        cost_estimate=pl.CostEstimate(
            flops=units * GROUP * rows * rows * 40 * PAIR,
            bytes_accessed=4 * n * rows * PAIR * heads,
            transcendentals=units * GROUP * rows * rows,
        ),
        name="attend_backward",
    )(place, kv, q_own, q_mirrored, do_own, do_mirrored, stats, gate, up, down)


def last_kernel(n, sizes, cuts, tall, first, gains, piece, out, acc, near, *rest):
    buffers, sems, rest = rest[:9], rest[9:14], rest[14:]
    near_gains, gain_sem, spread_send, spread_recv, home_sem = rest
    tree = TreeSum(n, sizes, cuts, acc, near, buffers, *sems)
    here = coordinates(n)
    x, y, z, core = here["x"], here["y"], here["z"], here["core"]
    partner = tree.partner
    greet([partner] + tree_peers(n, here, sizes))
    wide = acc.shape[4]
    sx, sy, sz, deep = acc.shape[:4]

    def pieces(of):
        return [
            (
                lambda x, c: first.at[pl.ds(pl.multiple_of(x * tall + c * 16, 16), 16), pl.ds(of * wide, wide)],
                0,
                wide,
            )
        ]

    wholes = [first.at[:, pl.ds(0, wide)]]
    to_partner = remote(gains, near_gains, gain_sem.at[0], gain_sem.at[1], partner)
    to_partner.start()
    tree.swap(pieces, tall)
    spans = ((wide, piece.shape[1]), (0, wide))

    def spread(kind, step):
        found = []
        for part in range(2):
            half = spans[kind][1] // 2
            columns = pl.ds(spans[kind][0] + part * half, half)
            axis = "yz"[(step + part) % 2]
            if step == 0:
                source = out.at[core, y, z, :, columns]
            elif axis == "z":
                source = out.at[core, :, z, :, columns]
            else:
                source = out.at[core, y, :, :, columns]
            found += [
                remote(
                    source, source, spread_send.at[kind, step, part, d], spread_recv.at[kind, step, part, d],
                    device_at(n, here, **{axis: peer}),
                )
                for d, peer in enumerate(peers_along(n, here, axis, sizes[axis]))
            ]
        return found

    def home(kind):
        half = out.at[core, :, :, :, pl.ds(*spans[kind])]
        return remote(half, half, home_sem.at[kind], home_sem.at[2 + kind], partner)

    def start(copies):
        for copy in copies:
            copy.start()

    def arrived(copies):
        for copy in copies:
            copy.wait_recv()

    out[core, y, z, :, pl.ds(wide, piece.shape[1])] = piece[...]
    start(spread(0, 0))
    tree.join(wholes, tall)
    to_partner.wait_recv()
    both = gains[...] + near_gains[...]
    row = tall % deep
    acc[:, tall // (deep * sz), (tall // deep) % sz, row : row + GAIN_ROWS, : gains.shape[2]] = both
    tree.start(0)
    arrived(spread(0, 0))
    start(spread(0, 1))
    tree.finish(0, True)
    tree.finish(1, True)
    tree.finish(2, False)
    out[core, y, z, :, pl.ds(0, wide)] = acc[x, y, z]
    start(spread(1, 0))
    arrived(spread(0, 1))
    home(0).start()
    arrived(spread(1, 0))
    start(spread(1, 1))
    arrived(spread(1, 1))
    home(1).start()
    arrived([home(0), home(1)])
    for kind in range(2):
        for copy in spread(kind, 0) + spread(kind, 1) + [home(kind)]:
            copy.wait_send()
    to_partner.wait_send()
    tree.sent_swap(wholes)
    tree.sent_steps()


def last_sums(first, gains, piece):
    n, sx = lax.axis_size("ctx"), lax.axis_size("wt")
    sy, sz = torus(n)
    tall = first.shape[0] // sx
    wide = first.shape[1] // 2
    sizes, cuts, blocks, buffers, sems = tree_layout(n, sx, tall, wide)
    deep = blocks[0].shape[3]
    peers = max(sy, sz, 2) - 1
    dma = pltpu.SemaphoreType.DMA
    inside = pl.BlockSpec(memory_space=pltpu.VMEM)
    out = pl.pallas_call(
        functools.partial(last_kernel, n, sizes, cuts, tall),
        out_shape=jax.ShapeDtypeStruct((2, sy, sz, deep, wide + piece.shape[1]), BF16),
        in_specs=[pl.BlockSpec(memory_space=pl.ANY), inside, inside],
        out_specs=inside,
        scratch_shapes=[
            *blocks, *buffers, *sems,
            pltpu.VMEM(gains.shape, BF16), dma((2,)), dma((2, 2, 2, peers)), dma((2, 2, 2, peers)), dma((4,)),
        ],
        compiler_params=pltpu.CompilerParams(
            collective_id=1, has_side_effects=True, vmem_limit_bytes=40 * 2**20
        ),
        name="last_sums",
    )(first, gains, piece)
    return out.reshape(2, sy * sz * deep, out.shape[4])


def rms_forward(values, gain):
    inverse = lax.rsqrt(jnp.mean(values * values, axis=-1, keepdims=True) + EPSILON)
    normal = values * inverse
    return (normal * gain, normal, inverse)


def rms_backward(upstream, gain, normal, inverse):
    scaled = upstream * gain
    inner = jnp.mean(scaled * normal, axis=-1, keepdims=True)
    return (inverse * (scaled - normal * inner), jnp.sum(upstream * normal, axis=0))


def positions_of(edges, me, rows):
    token = me * rows + jnp.arange(rows, dtype=jnp.int32)
    start = jnp.where(token >= edges[1], edges[1], jnp.where(token >= edges[0], edges[0], 0))
    return token, token - start


def turn(heads, cosine, sine):
    half = HEAD_SIZE // 2
    low, high = heads[:, :half], heads[:, half:]
    return jnp.concatenate([low * cosine - high * sine, high * cosine + low * sine], axis=1)


def turn_back(heads, cosine, sine):
    half = HEAD_SIZE // 2
    low, high = heads[:, :half], heads[:, half:]
    return jnp.concatenate([low * cosine + high * sine, high * cosine - low * sine], axis=1)


def three_parts(values):
    first = lax.reduce_precision(values, 8, 7)
    rest = values - first
    second = lax.reduce_precision(rest, 8, 7)
    third = rest - second
    return [part.astype(BF16) for part in (first, second, third)]


def joined(parts):
    return parts[0].astype(F32) + parts[1].astype(F32) + parts[2].astype(F32)


def gather_weight(shard):
    return lax.all_gather(shard, "wt", axis=0, tiled=True)


def per_device(
    layer_input,
    doc_bounds,
    attn_gain,
    w_query,
    key_weight,
    value_weight,
    w_out,
    mlp_gain,
    w_gate,
    w_up,
    w_down,
    cotangent,
):
    n = lax.axis_size("ctx")
    me = lax.axis_index("ctx")
    rows, width = layer_input.shape[1:]
    queries = QUERY_HEADS * HEAD_SIZE
    keys = KEY_VALUE_HEADS * HEAD_SIZE
    edges = doc_bounds[0]
    place = jnp.concatenate([jnp.full((1,), me, jnp.int32), edges])
    across = [(i, n - 1 - i) for i in range(n)]

    gains = jnp.pad(jnp.stack([attn_gain, mlp_gain], axis=1), ((0, 0), (0, 62)))
    shard_qkv = jnp.concatenate([w_query, key_weight, value_weight, gains], axis=1)
    full_qkv = gather_weight(shard_qkv)
    full_qkv, w_out, w_gate, w_up, w_down = lax.optimization_barrier((full_qkv, w_out, w_gate, w_up, w_down))
    gain_rows = full_qkv[:, queries + 2 * keys : queries + 2 * keys + 2].T.astype(F32)
    attn_scale, mlp_scale = gain_rows[0], gain_rows[1]
    full_qkv = full_qkv[:, : queries + 2 * keys]

    x = layer_input[0].astype(F32)
    normed, normal_in, inverse_in = rms_forward(x, attn_scale)
    normed = normed.astype(BF16)
    turned = dot_f32(full_qkv, normed, ((0,), (1,)))
    token, position = positions_of(edges, me, rows)
    freqs = 10000.0 ** (-jnp.arange(HEAD_SIZE // 2, dtype=F32) * 2.0 / HEAD_SIZE)
    angles = freqs[:, None] * position.astype(F32)[None, :]
    cosine, sine = jnp.cos(angles), jnp.sin(angles)

    q = turn(turned[:queries].reshape(QUERY_HEADS, HEAD_SIZE, rows), cosine, sine).astype(BF16)
    k = turn(turned[queries : queries + keys].reshape(KEY_VALUE_HEADS, HEAD_SIZE, rows), cosine, sine).astype(BF16)
    v = turned[queries + keys :].reshape(KEY_VALUE_HEADS, HEAD_SIZE, rows).astype(BF16)
    q = q * BF16(HEAD_SIZE**-0.5)
    own_kv = jnp.concatenate([k, v], axis=1).transpose(0, 2, 1)

    kv, mirrored = gather_blocks(own_kv, q)
    kv = kv.reshape(KEY_VALUE_HEADS, n * rows, PAIR)

    core = me % 2
    full_out = gather_weight(w_out)
    along_wide = lax.all_gather(jnp.where(core == 0, w_gate, w_up), "wt", axis=0)
    down_rows = w_down.shape[0] // 2
    along_down = lax.all_gather(lax.dynamic_slice_in_dim(w_down, core * down_rows, down_rows), "wt", axis=0)

    later = token >= edges[1]
    o_part, stat_part, sent = attention_forward(n, place, kv, q, mirrored)
    got, full_wide, full_down = exchange(sent, along_wide, along_down)
    full_wide = full_wide.reshape(2, width, -1)
    full_gate, full_up = full_wide[0], full_wide[1]
    full_down = full_down.reshape(-1, width)
    other_stat = joined([got[:, HEAD_SIZE + i : HEAD_SIZE + i + 1] for i in range(3)])
    other_stat = jnp.where(later, NEG, other_stat)
    log_total = jnp.logaddexp(stat_part, other_stat)
    attended = o_part * jnp.exp(stat_part - log_total) + got[:, :HEAD_SIZE].astype(F32) * jnp.exp(
        other_stat - log_total
    )
    mixed = attended.reshape(queries, rows).astype(BF16)

    resid = x + dot_f32(mixed, full_out, ((0,), (0,)))
    normed_two, normal_mlp, inverse_mlp = rms_forward(resid, mlp_scale)
    normed_two = normed_two.astype(BF16)
    gate = dot_f32(normed_two, full_gate)
    up = dot_f32(normed_two, full_up)
    sig = jax.nn.sigmoid(gate)
    activated = gate * sig
    hidden = (activated * up).astype(BF16)
    layer_output = (resid + dot_f32(hidden, full_down)).astype(BF16)[None]
    upstream = cotangent[0]
    grad_w_down = dot_f32(upstream, hidden, ((0,), (0,)))
    grad_hidden = dot_f32(upstream, full_down, ((1,), (1,)))
    grad_up_in = (grad_hidden * activated).astype(BF16)
    grad_gate_in = (grad_hidden * up * sig * (1.0 + gate * (1.0 - sig))).astype(BF16)
    grad_w_gate = dot_f32(normed_two, grad_gate_in, ((0,), (0,)))
    grad_w_up = dot_f32(normed_two, grad_up_in, ((0,), (0,)))
    grad_normed_two = dot_f32(grad_gate_in, full_gate, ((1,), (1,))) + dot_f32(
        grad_up_in, full_up, ((1,), (1,))
    )
    grad_resid_mlp, grad_mlp_gain = rms_backward(grad_normed_two, mlp_scale, normal_mlp, inverse_mlp)
    grad_resid = upstream.astype(F32) + grad_resid_mlp
    grad_mixed = grad_resid.astype(BF16)
    grad_w_out = dot_f32(mixed, grad_mixed)
    grad_attended = dot_f32(full_out, grad_mixed, ((1,), (1,))).astype(BF16)
    grad_attended = grad_attended.reshape(QUERY_HEADS, HEAD_SIZE, rows)
    grad_dot = jnp.sum(grad_attended.astype(F32) * attended, axis=1, keepdims=True)

    before = jnp.where(later, BIG, log_total)
    blank = jnp.zeros((QUERY_HEADS, TAIL - 6, rows), BF16)
    sent = jnp.concatenate([grad_attended] + three_parts(before) + three_parts(grad_dot) + [blank], axis=1)
    got = lax.ppermute(sent, "ctx", across)
    stats = jnp.concatenate([before, log_total, grad_dot], axis=1)
    dq, dkv, piece = attention_backward(
        n, place, kv, q, mirrored, grad_attended, got, stats,
        grad_w_gate.astype(BF16), grad_w_up.astype(BF16), grad_w_down.astype(BF16),
    )
    grad_q = turn_back(dq * HEAD_SIZE**-0.5, cosine, sine).astype(BF16)
    dkv = dkv.astype(F32).transpose(0, 2, 1)
    grad_k = turn_back(dkv[:, :HEAD_SIZE], cosine, sine).astype(BF16)
    grad_v = dkv[:, HEAD_SIZE:].astype(BF16)
    grad_qkv = jnp.concatenate(
        [grad_q.reshape(queries, rows), grad_k.reshape(keys, rows), grad_v.reshape(keys, rows)]
    )
    grad_w_qkv = dot_f32(normed, grad_qkv, ((0,), (1,)))
    grad_normed = dot_f32(grad_qkv, full_qkv, ((0,), (1,)))
    grad_in, grad_attn_gain = rms_backward(grad_normed, attn_scale, normal_in, inverse_in)
    input_grad = (grad_resid + grad_in)[None]

    sx = lax.axis_size("wt")
    tall = width // sx
    gains = jnp.stack([grad_attn_gain, grad_mlp_gain]).reshape(2, sx, tall).transpose(1, 0, 2)
    gains = jnp.pad(gains, ((0, 0), (0, GAIN_ROWS - 2), (0, -tall % 128))).astype(BF16)
    first = jnp.concatenate([grad_w_qkv.astype(BF16), grad_w_out.astype(BF16)], axis=1)
    sums = last_sums(first, gains, piece)
    wide = first.shape[1] // 2
    ff = w_gate.shape[1]
    block = ff // sx
    gain_sums = sums[0, tall : tall + 2, :tall].astype(F32)
    sums = sums[:, :tall].astype(F32)
    mixed_sums = jnp.concatenate([sums[0, :, :wide], sums[1, :, :wide]], axis=1)
    sum_down = jnp.concatenate(
        [sums[i, :, at : at + block] for i in range(2) for at in range(wide + ff, wide + ff + ff // 2, block)]
    ).T
    return (
        layer_output,
        input_grad,
        gain_sums[0],
        mixed_sums[:, :queries],
        mixed_sums[:, queries : queries + keys],
        mixed_sums[:, queries + keys : queries + 2 * keys],
        mixed_sums[:, queries + 2 * keys :],
        gain_sums[1],
        sums[0, :, wide : wide + ff],
        sums[1, :, wide : wide + ff],
        sum_down,
    )


def solution(mesh):
    tokens, weights, gains = P("wt", "ctx", None), P("wt", None), P("wt")
    return jax.shard_map(
        per_device,
        mesh=mesh,
        in_specs=(
            tokens, weights, gains, weights, weights, weights, weights, gains, weights, weights, weights, tokens,
        ),
        out_specs=(
            tokens, tokens, gains, weights, weights, weights, weights, gains, weights, weights, weights,
        ),
        check_vma=False,
    )
```
